256 devices in a mesh: dp: 32 (over x, y, core), mp: 8 (over z).
Axes of the slice: x: 4, y: 4, z: 8, core: 2. Of those that a mesh axis runs over, the one named last changes fastest.
Arguments:
- payload: bfloat16 [32, 512, 2, 10240], P('dp', None, None, 'mp'), may hold values from -6 to 6
- block_scale: float32 [32, 512, 2, 80], P('dp', None, None, 'mp'), may hold values from 0.25 to 4
- master: float32 [512, 2, 10240], P('dp', None, 'mp'), may hold values from -0.0006 to 0.0006
- moment_one: float32 [512, 2, 10240], P('dp', None, 'mp'), may hold values from -12 to 12
- moment_two: float32 [512, 2, 10240], P('dp', None, 'mp'), may hold values from 4 to 100
- owner: int32 [512, 1], P('dp'), may hold values from 0 to 31; in each aligned block of 16 rows (0 to 15, 16 to 31, ...) at most 2 rows name the same one
Outputs:
- new_master: float32 [512, 2, 10240], P('dp', None, 'mp')
- new_moment_one: float32 [512, 2, 10240], P('dp', None, 'mp')
- new_moment_two: float32 [512, 2, 10240], P('dp', None, 'mp')
- next_rows: bfloat16 [2048, 2, 10240], P(('dp', 'mp'))
The draws below stay inside these ranges and needn't reach their ends.
Inputs may be any that keep to these rules, and one draw needn't show every extreme that they name: Among the 16 rows of one device at most 2 name the same owner, and in every draw some device has exactly 2 rows naming one owner.
All inputs are finite; a program needn't handle non-finite values.
Results may differ from the reference program's by a relative error of at most 0.015.
Values may be sent and summed in bfloat16 or wider, within the bound.
A program may use at most 64 MiB of HBM per device.

```python
import math
import jax
import jax.numpy as jnp
import numpy as np
from jax import lax

QKV = 10240
BLOCK = 128
LAYERS = 2
STEP = 100
ROW_DEV = 16
REPLICAS = 32
ROWS = 512
CAP = 2
BLOCKS = 80
N_DP = 32


def raised(result, stream_key, source, target, shards_of, factor):
    def block_of(dim):
        return (jnp.arange(result.shape[dim]) // (result.shape[dim] // shards_of)).reshape((-1,) + (1,) * (result.ndim - 1 - dim))

    one_side = jax.random.permutation(stream_key, shards_of)[block_of(target)]
    other_side = (block_of(target) + shards_of // 2) % shards_of
    return jnp.where((block_of(source) == one_side) | (block_of(source) == other_side), factor * result, result)


def steps_of(rng, extent, cuts, least, top_value):
    factor_of, own = 1.0, jax.random.fold_in(rng, 6)
    for position, shards_of in cuts:
        steps = jnp.exp(jax.random.uniform(jax.random.fold_in(own, position), (shards_of,), jnp.float32, least / len(cuts), top_value / len(cuts)))
        factor_of = factor_of * jnp.repeat(steps, extent[position] // shards_of).reshape([-1 if axis == position else 1 for axis in range(len(extent))])
    return factor_of


def deal_out(own_key, own, number, rows, amount, top, bound, skew):
    ranking = jax.random.permutation(own_key, amount)
    crowded, common = portions_of(amount, rows * top, bound, skew, True), portions_of(amount, rows * top, bound, skew, False)
    places = jnp.arange(amount)

    def named(sizes, offset_by):
        used = int((sizes > 0).sum())
        fixed = max(1, used // 4)
        shifted = fixed + (places - fixed + offset_by * (used - fixed)) % max(1, amount - fixed)
        return jnp.zeros((amount,), jnp.int32).at[ranking[jnp.where(places < fixed, places, shifted)]].set(jnp.asarray(sizes, jnp.int32))

    sizes = jnp.where(number % 4 == 0, named(crowded, number // 4), named(common, number - number // 4 - 1))
    mixed = jax.random.permutation(jax.random.fold_in(own, 3), amount)
    giver, sink = mixed[0:amount // 2 * 2:2], mixed[1:amount // 2 * 2:2]
    margin = jnp.minimum(sizes[giver] - 1, bound - sizes[sink]) // 2
    margin = jnp.where((giver == ranking[0]) | (sink == ranking[0]) | (sizes[sink] == 0), 0, jnp.maximum(margin, 0))
    shifted = jax.random.randint(jax.random.fold_in(own, 4), (amount // 2,), 0, 1 << 20) % (margin + 1)
    sizes = sizes.at[giver].add(-shifted).at[sink].add(shifted)
    labels = jnp.searchsorted(jnp.cumsum(sizes), jnp.arange(rows * top), side="right").astype(jnp.int32)
    listing = labels.reshape(top, rows).T
    listing = listing[jax.random.permutation(jax.random.fold_in(own, 1), rows)]
    offset_by = jax.random.randint(jax.random.fold_in(own, 2), (rows, 1), 0, top)
    return jnp.take_along_axis(listing, (jnp.arange(top)[None, :] + offset_by) % top, axis=1)


def portions_of(amount, total, most, skew, full):
    weights = [(1 << 20) // math.isqrt(grade ** skew) + 1 for grade in range(1, amount + 1)]
    largest = most if full else min(most, max(-(-total // amount), total * weights[0] // sum(weights)))
    least = 1 if total - largest >= amount - 1 else 0
    counts, surplus = [largest] + [least] * (amount - 1), total - largest - least * (amount - 1)
    while surplus > 0:
        candidates = [i for i in range(1, amount) if counts[i] < largest] or [i for i in range(1, amount) if counts[i] < most]
        whole, remaining = sum([weights[i] for i in candidates]), surplus
        for i in candidates:
            more = min(most - counts[i], max(1, remaining * weights[i] // whole), surplus)
            counts[i] = counts[i] + more
            surplus = surplus - more
    return np.array(counts)


def bell_draw(own_key, extent, scale, reach, shards=(), held_as=jnp.bfloat16):
    loudness = steps_of(own_key, extent, shards, -0.22, 0.18) if shards else 1.0
    drawn = jax.random.normal(own_key, extent, jnp.float32) * scale * loudness
    return jnp.minimum(jnp.maximum(drawn, -reach), reach).astype(held_as)


def bell_draw_with(stream_key, extent, deviation, reach, pieces, heavy, kind=jnp.bfloat16):
    array = deviation * jax.random.normal(stream_key, extent, jnp.float32)
    if pieces:
        array = array * steps_of(stream_key, extent, pieces, -0.22, 0.18)
    return jnp.clip(raised(array, jax.random.fold_in(stream_key, 3), *heavy), -reach, reach).astype(kind)


def setup_inputs(seed: int = 0) -> dict:
    streams_of = jax.random.split(jax.random.key(seed), 7)
    payload = bell_draw_with(streams_of[0], (REPLICAS, ROWS, LAYERS, QKV), 1.0, 6.0, ((0, 32), (3, 8)), (0, 1, 32, 2.75))
    block_scale = jnp.clip(jnp.exp(math.log(4.0) - 2.7725887 * jax.random.uniform(streams_of[1], (REPLICAS, ROWS, LAYERS, BLOCKS), jnp.float32) ** steps_of(streams_of[1], (REPLICAS, ROWS, LAYERS, BLOCKS), ((0, 32), (3, 8)), -0.2, 0.2)), 0.25, 4.0)
    master = bell_draw(streams_of[2], (ROWS, LAYERS, QKV), (1e-4), 0.0006, ((0, 32), (2, 8)), jnp.float32)
    moment_one = bell_draw(streams_of[3], (ROWS, LAYERS, QKV), 2.0, 12.0, ((0, 32), (2, 8)), jnp.float32)
    moment_two = jnp.clip(jnp.exp(math.log(100.0) - 3.218876 * jax.random.uniform(streams_of[4], (ROWS, LAYERS, QKV), jnp.float32) ** steps_of(streams_of[4], (ROWS, LAYERS, QKV), ((0, 32), (2, 8)), -0.2, 0.2)), 4.0, 100.0)
    owner_keys = jax.random.split(jax.random.fold_in(streams_of[5], 1), ROWS // ROW_DEV)
    owner_turns = jax.random.permutation(jax.random.fold_in(streams_of[5], 3), ROWS // ROW_DEV)
    owner = jax.vmap(lambda own, number: deal_out(jax.random.fold_in(streams_of[5], 2), own, number, ROW_DEV, N_DP, 1, CAP, 1))(owner_keys, owner_turns).reshape((ROWS, 1))
    return {"payload": payload, "block_scale": block_scale, "master": master, "moment_one": moment_one, "moment_two": moment_two, "owner": owner}


def dequantize(values, scales):
    shape = values.shape
    blocks = values.astype(jnp.float32).reshape(shape[:-1] + (scales.shape[-1], BLOCK))
    return (blocks * scales[..., None]).reshape(shape)

def reference(payload, block_scale, master, moment_one, moment_two, owner):

    def accumulate(index, total):
        values = lax.dynamic_index_in_dim(payload, index, 0, keepdims=False)
        scales = lax.dynamic_index_in_dim(block_scale, index, 0, keepdims=False)
        return total + dequantize(values, scales)
    grad = lax.fori_loop(0, REPLICAS, accumulate, jnp.zeros(master.shape, jnp.float32))
    step_count = STEP + 1
    new_moment_one = 0.9 * moment_one + 0.1 * grad
    new_moment_two = 0.95 * moment_two + 0.05 * grad * grad
    first_fix = 1.0 - 0.9 ** step_count
    second_fix = 1.0 - 0.95 ** step_count
    direction = new_moment_one / first_fix / (jnp.sqrt(new_moment_two / second_fix) + 1e-08)
    new_master = master - 0.00015 * (direction + 0.1 * master)
    rounded = new_master.astype(jnp.bfloat16)
    owners = owner[:, 0].reshape(N_DP, ROW_DEV)
    same = owners[:, :, None] == owners[:, None, :]
    earlier = jnp.arange(ROW_DEV)[:, None] > jnp.arange(ROW_DEV)[None, :]
    rank = lax.optimization_barrier(jnp.sum((same & earlier[None]).astype(jnp.int32), axis=2))
    source = jnp.arange(N_DP, dtype=jnp.int32)[:, None]
    target = (owners * (N_DP * CAP) + source * CAP + rank).astype(jnp.int32).reshape(-1)
    next_rows = jnp.zeros((N_DP * N_DP * CAP, LAYERS, QKV), jnp.bfloat16).at[target].set(rounded)
    return (new_master, new_moment_one, new_moment_two, next_rows)
```

```python
import jax
import jax.numpy as jnp
from jax import lax
from jax.experimental import pallas as pl
from jax.experimental.pallas import tpu as pltpu
from jax.sharding import PartitionSpec as P

STEP = 100
ROWS = 16
TILES = 10
SIDE = 4
DEPTH = 8
NDP = 32
KEYS = 64
MESH = pl.DeviceIdType.MESH
BF16 = jnp.bfloat16
F32 = jnp.float32
GROUPS = ((0, 0, 5), (1, 5, 5))
CHUNKS = ((0, 10, (0, 1)),)
OFFSETS = (2, 1, 3, 0)


def iota(shape, dim):
    return lax.broadcasted_iota(jnp.int32, shape, dim)


def scratch():
    made = {
        "pay": pltpu.VMEM((NDP, TILES, ROWS, 2, 128), BF16),
        "scale": pltpu.VMEM((TILES, 2, 512), F32),
        "keys": pltpu.VMEM((2 * NDP * ROWS, KEYS), BF16),
        "state_in": pltpu.VMEM((3, TILES, ROWS, 2, 128), F32),
        "state": pltpu.VMEM((3, TILES, 32, 128), F32),
        "fresh": pltpu.VMEM((3, TILES, 32, 128), F32),
        "rounded": pltpu.VMEM((TILES, 32, 128), BF16),
        "owner": pltpu.VMEM((1, ROWS), jnp.int32),
        "load_sem": pltpu.SemaphoreType.DMA((TILES,)),
        "scale_sem": pltpu.SemaphoreType.DMA((2,)),
        "state_sem": pltpu.SemaphoreType.DMA((3, TILES)),
        "fresh_sem": pltpu.SemaphoreType.DMA,
    }
    for g, (_, _, n) in enumerate(GROUPS):
        block = (n, 32, 128)
        made |= {
            f"give{g}": pltpu.VMEM((SIDE, SIDE) + block, BF16),
            f"take{g}": pltpu.VMEM((SIDE, SIDE) + block, BF16),
            f"own{g}": pltpu.VMEM((SIDE, SIDE) + block, F32),
            f"first{g}": pltpu.VMEM((3, SIDE) + block, BF16),
            f"first_in{g}": pltpu.VMEM((3, SIDE) + block, BF16),
            f"second{g}": pltpu.VMEM((3,) + block, BF16),
            f"second_in{g}": pltpu.VMEM((3,) + block, BF16),
            f"total{g}": pltpu.VMEM(block, F32),
            f"pair_sem{g}": pltpu.SemaphoreType.DMA((2, 4)),
            f"first_sem{g}": pltpu.SemaphoreType.DMA((2, 3)),
            f"second_sem{g}": pltpu.SemaphoreType.DMA((2, 3)),
        }
    for h, (_, n, _) in enumerate(CHUNKS):
        made |= {
            f"select{h}": pltpu.VMEM((128 * n, 32 * n), BF16),
            f"slots{h}": pltpu.VMEM((NDP, 4 * n, 128), BF16),
            f"plane{h}": pltpu.VMEM((DEPTH, 4, 4 * n, 128), BF16),
            f"plane_sem{h}": pltpu.SemaphoreType.DMA((2, NDP)),
            f"deep_sem{h}": pltpu.SemaphoreType.DMA((2, DEPTH)),
        }
    return made


NAMES = tuple(scratch())


def kernel(pay_in, scale_in, master_in, one_in, two_in, owner_in, *rest):
    fresh_out, next_out = rest[0], rest[1:1 + len(CHUNKS)]
    r = dict(zip(NAMES, rest[1 + len(CHUNKS):]))
    dp, z = lax.axis_index("dp"), lax.axis_index("mp")
    c, y, x = dp % 2, dp // 2 % SIDE, dp // (2 * SIDE)

    def place(px, py, pc):
        return (px * SIDE + py) * 2 + pc

    def signal(device):
        pl.semaphore_signal(barrier, inc=1, device_id=device, device_id_type=MESH)

    def remote(src, dst, sems, i, j, device):
        return pltpu.make_async_remote_copy(
            src, dst, sems.at[0, i], sems.at[1, j], device_id=device, device_id_type=MESH
        )

    barrier = pltpu.get_barrier_semaphore()

    def greet_plane(i, carry):
        signal(((dp + i) % NDP, z))
        return carry

    def greet_depth(i, carry):
        signal((dp, (z + i) % DEPTH))
        return carry

    lax.fori_loop(1, NDP, greet_plane, 0)
    lax.fori_loop(1, DEPTH, greet_depth, 0)

    scale_load = pltpu.make_async_copy(scale_in, r["scale"], r["scale_sem"].at[0])
    owner_load = pltpu.make_async_copy(owner_in, r["owner"], r["scale_sem"].at[1])
    loads = [
        pltpu.make_async_copy(pay_in.at[:, :, t], r["pay"].at[:, t], r["load_sem"].at[t])
        for t in range(TILES)
    ]
    state_loads = [
        pltpu.make_async_copy(ref.at[:, t], r["state_in"].at[i, t], r["state_sem"].at[i, t])
        for i, ref in enumerate((master_in, one_in, two_in))
        for t in range(TILES)
    ]
    for copy in [scale_load, owner_load] + loads + state_loads:
        copy.start()

    scale_load.wait()
    spread = (iota((256, 128), 0) // 2 == iota((256, 128), 1)).astype(BF16)
    match = iota((256, KEYS), 0) % 2 == iota((256, KEYS), 1) // 10 % 2

    for k in range(4):
        whole = [r["scale"][:, i, 128 * k : 128 * k + 128] for i in range(2)]
        parts = []
        for _ in range(3):
            part = [value.astype(BF16).astype(F32) for value in whole]
            whole = [value - near for value, near in zip(whole, part)]
            parts += part
        parts = jnp.concatenate(parts + [jnp.zeros((KEYS - 60, 128), F32)], axis=0)
        turned = lax.dot_general(
            spread, parts.astype(BF16), (((1,), (1,)), ((), ())), preferred_element_type=F32
        )
        r["keys"][256 * k : 256 * k + 256, :] = jnp.where(match, turned, 0.0).astype(BF16)

    owner_load.wait()
    targets = r["owner"][...].astype(F32)
    square = (ROWS, ROWS)
    diagonal = jnp.where(iota(square, 0) == iota(square, 1), jnp.broadcast_to(targets, square), 0.0)
    columns = jnp.dot(diagonal.astype(BF16), jnp.ones(square, BF16), preferred_element_type=F32)
    earlier = (columns == targets) & (iota(square, 0) < iota(square, 1))
    rank = jnp.sum(jnp.where(earlier, 1.0, 0.0), axis=0, keepdims=True)
    slot = jnp.broadcast_to(targets * 2.0 + rank, (8, ROWS)).astype(BF16)
    for h, (_, n, _) in enumerate(CHUNKS):
        wide = (ROWS, 32 * n)
        repeat = (iota(wide, 1) % 32 // 2 == iota(wide, 0)).astype(BF16)
        slots = jnp.dot(slot, repeat, preferred_element_type=F32)[0:1]
        line = iota((1, 32 * n), 1)
        goal = slots.astype(jnp.int32) * (2 * n) + line // 32 * 2 + line % 2
        r[f"select{h}"][...] = (iota((128 * n, 32 * n), 0) == goal).astype(BF16)

    for copy in loads:
        copy.wait()
    centre = ((x, y), (y, x))

    def block_of(g, a, b, core):
        return place(a, b, core) if GROUPS[g][0] == 0 else place(b, a, core)

    widen = []
    for _, t0, n in GROUPS:
        shape = (KEYS, 128 * n)
        widen.append((iota(shape, 0) % 10 == iota(shape, 1) // 128 + t0).astype(BF16))

    def terms(g, a, b, core):
        _, t0, n = GROUPS[g]
        block = block_of(g, a, b, core)
        keys = r["keys"][pl.ds(pl.multiple_of(32 * block, 32), 32), :]
        scales = jnp.dot(keys, widen[g], preferred_element_type=F32)
        for t in range(n):
            values = r["pay"][block, t0 + t].reshape(32, 128).astype(F32)
            yield t, values * scales[:, 128 * t : 128 * t + 128]

    for g in range(len(GROUPS)):

        def give(i, carry, g=g):
            a, b = i // SIDE, i % SIDE
            for t, term in terms(g, a, b, 1 - c):
                r[f"give{g}"][a, b, t] = term.astype(BF16)
            return carry

        lax.fori_loop(0, SIDE * SIDE, give, 0)
    for g in range(len(GROUPS)):

        def keep(i, carry, g=g):
            a, b = i // SIDE, i % SIDE
            for t, term in terms(g, a, b, c):
                r[f"own{g}"][a, b, t] = term
            return carry

        lax.fori_loop(0, SIDE * SIDE, keep, 0)

    for copy in state_loads:
        copy.wait()

    def turn(t, carry):
        for i in range(3):
            r["state"][i, t] = r["state_in"][i, t].reshape(32, 128)
        return carry

    lax.fori_loop(0, TILES, turn, 0)
    pl.semaphore_wait(barrier, NDP - 1 + DEPTH - 1)

    pair = {}
    for k in range(4):
        for g, (axis, _, _) in enumerate(GROUPS):
            a = (centre[axis][0] + OFFSETS[k]) % SIDE
            pair[g, k] = remote(
                r[f"give{g}"].at[a],
                r[f"take{g}"].at[a],
                r[f"pair_sem{g}"],
                k,
                k,
                (place(x, y, 1 - c), z),
            )
            pair[g, k].start()
    first = {}
    for k in range(4):
        for g, (axis, _, n) in enumerate(GROUPS):
            a = (centre[axis][0] + OFFSETS[k]) % SIDE
            pair[g, k].wait_recv()

            def add(b, carry, g=g, n=n, k=k, a=a):
                for t in range(n):
                    total = r[f"own{g}"][a, b, t] + r[f"take{g}"][
                        a, b, t
                    ].astype(F32)
                    if k < 3:
                        r[f"first{g}"][k, b, t] = total.astype(BF16)
                    else:
                        r[f"own{g}"][a, b, t] = total
                return carry

            lax.fori_loop(0, SIDE, add, 0)
            if k < 3:
                there = place(a, y, c) if axis == 0 else place(x, a, c)
                first[g, k] = remote(
                    r[f"first{g}"].at[k], r[f"first_in{g}"].at[k], r[f"first_sem{g}"], k, k, (there, z)
                )
                first[g, k].start()
    second = {}
    for g, (axis, _, n) in enumerate(GROUPS):
        a, b0 = centre[axis]
        for k in range(3):
            first[g, k].wait_recv()
        for k in range(4):
            b = (b0 + OFFSETS[k]) % SIDE
            for t in range(n):
                total = r[f"own{g}"][a, b, t]
                for j in range(3):
                    total += r[f"first_in{g}"][j, b, t].astype(F32)
                if k < 3:
                    r[f"second{g}"][k, t] = total.astype(BF16)
                else:
                    r[f"total{g}"][t] = total
            if k < 3:
                there = place(x, b, c) if axis == 0 else place(b, y, c)
                second[g, k] = remote(
                    r[f"second{g}"].at[k],
                    r[f"second_in{g}"].at[k],
                    r[f"second_sem{g}"],
                    k,
                    k,
                    (there, z),
                )
                second[g, k].start()
    stores = []
    fix_one = 1.0 - 0.9 ** (STEP + 1)
    fix_two = 1.0 - 0.95 ** (STEP + 1)
    for h, (h0, hn, members) in enumerate(CHUNKS):
        for g in members:
            _, t0, n = GROUPS[g]
            for k in range(3):
                second[g, k].wait_recv()
            for t in range(n):
                grad = r[f"total{g}"][t]
                for j in range(3):
                    grad += r[f"second_in{g}"][j, t].astype(F32)
                master, one, two = (
                    r["state"][i, t0 + t] for i in range(3)
                )
                one = 0.9 * one + 0.1 * grad
                two = 0.95 * two + 0.05 * grad * grad
                direction = one / fix_one / (jnp.sqrt(two / fix_two) + 1e-08)
                master = master - 0.00015 * (direction + 0.1 * master)
                for i, value in enumerate((master, one, two)):
                    r["fresh"][i, t0 + t] = value
                r["rounded"][t0 + t] = master.astype(BF16)
        rows = r["rounded"][h0 : h0 + hn].reshape(32 * hn, 128)
        moved = jnp.dot(r[f"select{h}"][...], rows, preferred_element_type=F32)
        r[f"slots{h}"][...] = moved.reshape(NDP, 4 * hn, 128).astype(BF16)

        def send(i, carry, h=h):
            d = (dp + i) % NDP
            remote(
                r[f"slots{h}"].at[d], r[f"plane{h}"].at[dp // 4, dp % 4], r[f"plane_sem{h}"], i, i, (d, z)
            ).start()
            return carry

        lax.fori_loop(1, NDP, send, 0)
        stay = pltpu.make_async_copy(
            r[f"slots{h}"].at[dp], r[f"plane{h}"].at[dp // 4, dp % 4], r[f"plane_sem{h}"].at[0, 0]
        )
        stay.start()
        def land(i, carry, h=h):
            d = (dp + NDP - i) % NDP
            remote(
                r[f"slots{h}"].at[d], r[f"plane{h}"].at[d // 4, d % 4], r[f"plane_sem{h}"], i, i, (d, z)
            ).wait_recv()
            return carry

        lax.fori_loop(1, NDP, land, 0)
        stay.wait()
    copy = pltpu.make_async_copy(r["fresh"], fresh_out, r["fresh_sem"])
    copy.start()
    stores.append(copy)
    deep, own = [], []
    for h, (h0, hn, _) in enumerate(CHUNKS):
        there = next_out[h].at[z]
        grouped = r[f"plane{h}"]
        for i in (4, 3, 5, 2, 6, 1, 7):
            to = (z + i) % DEPTH
            copy = remote(grouped.at[to], there, r[f"deep_sem{h}"], i, i, (dp, to))
            copy.start()
            deep.append(copy)
        copy = pltpu.make_async_copy(grouped.at[z], there, r[f"deep_sem{h}"].at[0, 0])
        copy.start()
        own.append(copy)
    for copy in list(pair.values()) + list(first.values()) + list(second.values()):
        copy.wait_send()
    for h in range(len(CHUNKS)):

        def sent(i, carry, h=h):
            d = (dp + i) % NDP
            remote(
                r[f"slots{h}"].at[d], r[f"plane{h}"].at[dp // 4, dp % 4], r[f"plane_sem{h}"], i, i, (d, z)
            ).wait_send()
            return carry

        lax.fori_loop(1, NDP, sent, 0)
    for copy in stores + own + deep:
        copy.wait()


def finish(fresh, *rest):
    parts = len(CHUNKS)
    arrived, outs, rows_out = rest[:parts], rest[parts : parts + 3], rest[parts + 3]
    state, state_in_sem, state_sem, rows_in_sem, rows_sem = rest[parts + 4 : parts + 9]
    rows = rest[parts + 9 :]
    loads = [pltpu.make_async_copy(fresh, state, state_in_sem)]
    loads += [pltpu.make_async_copy(arrived[h], rows[h], rows_in_sem.at[h]) for h in range(parts)]
    for copy in loads:
        copy.start()
    copies = []

    def store(src, dst, sem):
        copies.append(pltpu.make_async_copy(src, dst, sem))
        copies[-1].start()

    loads[0].wait()
    for i in range(3):
        for t in range(TILES):
            store(state.at[i, t], outs[i].at[:, t], state_sem.at[i, t])
    for h, (h0, n, _) in enumerate(CHUNKS):
        loads[1 + h].wait()
        for m in range(DEPTH):
            store(rows[h].at[m], rows_out.at[:, pl.ds(m * TILES + h0, n)], rows_sem.at[h, m])
    for copy in copies:
        copy.wait()


def body(payload, block_scale, master, moment_one, moment_two, owner):
    def fold(array):
        split = array.shape[:-1] + (array.shape[-1] // 128, 128)
        return jnp.swapaxes(array.reshape(split), -3, -2)

    def unfold(array):
        array = jnp.swapaxes(array, -3, -2)
        return array.reshape(array.shape[:-2] + (-1,))

    anywhere = pl.BlockSpec(memory_space=pl.ANY)
    fresh, *arrived = pl.pallas_call(
        kernel,
        out_shape=(
            jax.ShapeDtypeStruct((3, TILES, 32, 128), F32),
            *(jax.ShapeDtypeStruct((DEPTH, 4, 4 * n, 128), BF16) for _, n, _ in CHUNKS),
        ),
        in_specs=[anywhere] * 6,
        out_specs=(anywhere,) * (1 + len(CHUNKS)),
        scratch_shapes=list(scratch().values()),
        compiler_params=pltpu.CompilerParams(
            collective_id=0, has_side_effects=True, vmem_limit_bytes=60 * 2**20
        ),
    )(
        fold(payload[0].reshape(NDP, ROWS, 2, -1)),
        jnp.transpose(block_scale[0], (2, 1, 0)),
        fold(master),
        fold(moment_one),
        fold(moment_two),
        owner.T,
    )
    state = jax.ShapeDtypeStruct((ROWS, TILES, 2, 128), F32)
    results = pl.pallas_call(
        finish,
        out_shape=(state, state, state, jax.ShapeDtypeStruct((8, DEPTH * TILES, 2, 128), BF16)),
        in_specs=[anywhere] * (1 + len(CHUNKS)),
        out_specs=(anywhere,) * 4,
        scratch_shapes=[
            pltpu.VMEM((3, TILES, ROWS, 2, 128), F32),
            pltpu.SemaphoreType.DMA,
            pltpu.SemaphoreType.DMA((3, TILES)),
            pltpu.SemaphoreType.DMA((len(CHUNKS),)),
            pltpu.SemaphoreType.DMA((len(CHUNKS), DEPTH)),
            *(pltpu.VMEM((DEPTH, 8, n, 2, 128), BF16) for _, n, _ in CHUNKS),
        ],
    )(
        fresh.reshape(3, TILES, ROWS, 2, 128),
        *(part.reshape(DEPTH, 8, n, 2, 128) for part, (_, n, _) in zip(arrived, CHUNKS)),
    )
    return tuple(unfold(result) for result in results)


def solution(mesh):
    return jax.shard_map(
        body,
        mesh=mesh,
        in_specs=(
            P("dp", None, None, "mp"),
            P("dp", None, None, "mp"),
            P("dp", None, "mp"),
            P("dp", None, "mp"),
            P("dp", None, "mp"),
            P("dp", None),
        ),
        out_specs=(
            P("dp", None, "mp"),
            P("dp", None, "mp"),
            P("dp", None, "mp"),
            P(("dp", "mp"), None, None),
        ),
        check_vma=False,
    )
```

```python
import jax
import jax.numpy as jnp
from jax import lax
from jax.experimental import pallas as pl
from jax.experimental.layout import Layout, with_layout_constraint
from jax.experimental.pallas import tpu as pltpu
from jax.sharding import PartitionSpec as P

STEP = 100
ROWS = 16
TILES = 10
LINES = ROWS * TILES * 2
HALF = LINES // 2
SIDE = 4
CHIPS = SIDE * SIDE
DEPTH = 8
NDP = 32
KEYS = 64
MESH = pl.DeviceIdType.MESH
BF16 = jnp.bfloat16
F32 = jnp.float32
GROUPS = (0, 1)
CHUNKS = ((0, 10),)
OFFSETS = (2, 1, 3, 0)


def iota(shape, dim):
    return lax.broadcasted_iota(jnp.int32, shape, dim)


def scratch():
    made = {
        "scale": pltpu.VMEM((2, TILES, 2, 512), F32),
        "keys": pltpu.VMEM((2, CHIPS, 2, ROWS, KEYS), BF16),
        "spread": pltpu.VMEM((2, CHIPS, LINES, 128), F32),
        "state": pltpu.VMEM((3, LINES, 128), F32),
        "fresh": pltpu.VMEM((3, LINES, 128), F32),
        "rounded": pltpu.VMEM((LINES, 128), BF16),
        "owner": pltpu.VMEM((1, ROWS), jnp.int32),
        "load_sem": pltpu.SemaphoreType.DMA((2,)),
        "scale_sem": pltpu.SemaphoreType.DMA((4,)),
        "state_sem": pltpu.SemaphoreType.DMA((3,)),
        "fresh_sem": pltpu.SemaphoreType.DMA,
    }
    block = (HALF, 128)
    for g in GROUPS:
        made |= {
            f"mine{g}": pltpu.VMEM((SIDE, SIDE) + block, BF16),
            f"take{g}": pltpu.VMEM((SIDE, SIDE) + block, BF16),
            f"own{g}": pltpu.VMEM((SIDE,) + block, F32),
            f"first{g}": pltpu.VMEM((3, SIDE) + block, BF16),
            f"first_in{g}": pltpu.VMEM((3, SIDE) + block, BF16),
            f"second{g}": pltpu.VMEM((3,) + block, BF16),
            f"second_in{g}": pltpu.VMEM((3,) + block, BF16),
            f"total{g}": pltpu.VMEM(block, F32),
            f"pair_sem{g}": pltpu.SemaphoreType.DMA((2, 4)),
            f"first_sem{g}": pltpu.SemaphoreType.DMA((2, 3)),
            f"second_sem{g}": pltpu.SemaphoreType.DMA((2, 3)),
        }
    for h, (_, n) in enumerate(CHUNKS):
        made |= {
            f"select{h}": pltpu.VMEM((128 * n, LINES), BF16),
            f"slots{h}": pltpu.VMEM((NDP, 4 * n, 128), BF16),
            f"plane{h}": pltpu.VMEM((DEPTH, 4, 4 * n, 128), BF16),
            f"plane_sem{h}": pltpu.SemaphoreType.DMA((2, NDP)),
            f"deep_sem{h}": pltpu.SemaphoreType.DMA((2, DEPTH)),
        }
    return made


NAMES = tuple(scratch())


def kernel(pay_in, scale_in, master_in, one_in, two_in, owner_in, *rest):
    fresh_out, next_out = rest[0], rest[1 : 1 + len(CHUNKS)]
    r = dict(zip(NAMES, rest[1 + len(CHUNKS) :]))
    dp, z = lax.axis_index("dp"), lax.axis_index("mp")
    c, y, x = dp % 2, dp // 2 % SIDE, dp // (2 * SIDE)
    centre = ((x, y), (y, x))

    def place(px, py, pc):
        return (px * SIDE + py) * 2 + pc

    def near(g, a):
        return (place(a, y, c), z) if g == 0 else (place(x, a, c), z)

    def remote(src, dst, sems, i, j, device):
        return pltpu.make_async_remote_copy(
            src, dst, sems.at[0, i], sems.at[1, j], device_id=device, device_id_type=MESH
        )

    sibling = (place(x, y, 1 - c), z)
    greeted = [sibling]
    greeted += [near(g, (centre[g][0] + i) % SIDE) for i in range(1, SIDE) for g in GROUPS]
    greeted += [(dp, (z + i) % DEPTH) for i in range(1, DEPTH)]
    barrier = pltpu.get_barrier_semaphore()
    for device in greeted:
        pl.semaphore_signal(barrier, inc=1, device_id=device, device_id_type=MESH)

    scale_load = pltpu.make_async_copy(scale_in, r["scale"].at[0], r["scale_sem"].at[0])
    scale_load.start()
    owner_load = pltpu.make_async_copy(owner_in, r["owner"], r["scale_sem"].at[1])
    owner_load.start()
    loads = [
        pltpu.make_async_copy(
            pay_in.at[:, :, c, pl.ds(HALF * g, HALF)], r[f"mine{g}"], r["load_sem"].at[g]
        )
        for g in GROUPS
    ]
    state_loads = [
        pltpu.make_async_copy(ref, r["state"].at[i], r["state_sem"].at[i])
        for i, ref in enumerate((master_in, one_in, two_in))
    ]
    for copy in loads + state_loads:
        copy.start()
    pl.semaphore_wait(barrier, len(greeted))

    scale_pair = pltpu.make_async_remote_copy(
        scale_in,
        r["scale"].at[1],
        r["scale_sem"].at[2],
        r["scale_sem"].at[3],
        device_id=sibling,
        device_id_type=MESH,
    )
    scale_pair.start()
    pair = {}
    for k in range(4):
        for g in GROUPS:
            a = (centre[g][0] + OFFSETS[k]) % SIDE
            lines = pl.ds(HALF * g, HALF)
            source = pay_in.at[a, :, 1 - c, lines] if g == 0 else pay_in.at[:, a, 1 - c, lines]
            target = r[f"take{g}"].at[a] if g == 0 else r[f"take{g}"].at[:, a]
            pair[g, k] = remote(source, target, r[f"pair_sem{g}"], k, k, sibling)
            pair[g, k].start()

    eye = (iota((128, 128), 0) == iota((128, 128), 1)).astype(BF16)
    repeat = (iota((2 * LINES, 2 * ROWS), 0) // (2 * TILES) == iota((2 * LINES, 2 * ROWS), 1)).astype(
        BF16
    )
    line = iota((2 * LINES, KEYS), 0) % (2 * TILES)
    match = iota((2 * LINES, KEYS), 1) % (2 * TILES) == line % 2 * TILES + line // 2
    ones = jnp.ones((KEYS, 128), BF16)

    def spread(core):
        for k in range(4):
            whole = [r["scale"][core, :, i, 128 * k : 128 * k + 128] for i in range(2)]
            parts = []
            for _ in range(3):
                part = [value.astype(BF16).astype(F32) for value in whole]
                whole = [value - close for value, close in zip(whole, part)]
                parts += part
            parts = jnp.concatenate(parts + [jnp.zeros((KEYS - 60, 128), F32)], axis=0)
            turned = lax.dot_general(
                eye, parts.astype(BF16), (((1,), (1,)), ((), ())), preferred_element_type=F32
            )
            r["keys"][core, 4 * k : 4 * k + 4] = turned.astype(BF16).reshape(4, 2, ROWS, KEYS)

        def widen(i, carry):
            keys = r["keys"][core, pl.ds(2 * i, 2), c].reshape(2 * ROWS, KEYS)
            many = jnp.dot(repeat, keys, preferred_element_type=F32)
            many = jnp.where(match, many, 0.0).astype(BF16)
            wide = jnp.dot(many, ones, preferred_element_type=F32)
            r["spread"][core, pl.ds(2 * i, 2)] = wide.reshape(2, LINES, 128)
            return carry

        lax.fori_loop(0, CHIPS // 2, widen, 0)

    scale_load.wait()
    spread(0)
    scale_pair.wait_recv()
    spread(1)
    for copy in loads:
        copy.wait()

    first = {}
    for k in range(4):
        for g in GROUPS:
            a = (centre[g][0] + OFFSETS[k]) % SIDE
            pair[g, k].wait_recv()

            def add(b, carry, g=g, k=k, a=a):
                i, j = (a, b) if g == 0 else (b, a)
                lines = slice(HALF * g, HALF * g + HALF)
                total = r[f"mine{g}"][i, j].astype(F32) * r["spread"][0, i * SIDE + j, lines]
                total += r[f"take{g}"][i, j].astype(F32) * r["spread"][1, i * SIDE + j, lines]
                if k < 3:
                    r[f"first{g}"][k, b] = total.astype(BF16)
                else:
                    r[f"own{g}"][b] = total
                return carry

            lax.fori_loop(0, SIDE, add, 0)
            if k < 3:
                first[g, k] = remote(
                    r[f"first{g}"].at[k],
                    r[f"first_in{g}"].at[k],
                    r[f"first_sem{g}"],
                    k,
                    k,
                    near(g, a),
                )
                first[g, k].start()

    owner_load.wait()
    targets = r["owner"][...].astype(F32)
    square = (ROWS, ROWS)
    diagonal = jnp.where(iota(square, 0) == iota(square, 1), jnp.broadcast_to(targets, square), 0.0)
    columns = jnp.dot(diagonal.astype(BF16), jnp.ones(square, BF16), preferred_element_type=F32)
    earlier = (columns == targets) & (iota(square, 0) < iota(square, 1))
    rank = jnp.sum(jnp.where(earlier, 1.0, 0.0), axis=0, keepdims=True)
    slot = jnp.broadcast_to(targets * 2.0 + rank, (8, ROWS)).astype(BF16)
    wide = (ROWS, LINES)
    stretch = (iota(wide, 1) // (2 * TILES) == iota(wide, 0)).astype(BF16)
    slot = jnp.dot(slot, stretch, preferred_element_type=F32)[0:1].astype(jnp.int32)
    line = iota((1, LINES), 1) % (2 * TILES)
    for h, (h0, n) in enumerate(CHUNKS):
        inside = (line >= 2 * h0) & (line < 2 * h0 + 2 * n)
        goal = jnp.where(inside, slot * (2 * n) + line - 2 * h0, -1)
        r[f"select{h}"][...] = (iota((128 * n, LINES), 0) == goal).astype(BF16)
    for copy in state_loads:
        copy.wait()

    second = {}
    for g in GROUPS:
        a, b0 = centre[g]
        for k in range(3):
            first[g, k].wait_recv()
        for k in range(4):
            b = (b0 + OFFSETS[k]) % SIDE
            total = r[f"own{g}"][b]
            for j in range(3):
                total += r[f"first_in{g}"][j, b].astype(F32)
            if k == 3:
                r[f"total{g}"][...] = total
                continue
            r[f"second{g}"][k] = total.astype(BF16)
            second[g, k] = remote(
                r[f"second{g}"].at[k],
                r[f"second_in{g}"].at[k],
                r[f"second_sem{g}"],
                k,
                k,
                near(1 - g, b),
            )
            second[g, k].start()

    fix_one = 1.0 - 0.9 ** (STEP + 1)
    fix_two = 1.0 - 0.95 ** (STEP + 1)
    for g in GROUPS:
        for k in range(3):
            second[g, k].wait_recv()
        lines = slice(HALF * g, HALF * g + HALF)
        grad = r[f"total{g}"][...]
        for j in range(3):
            grad += r[f"second_in{g}"][j].astype(F32)
        master, one, two = (r["state"][i, lines] for i in range(3))
        one = 0.9 * one + 0.1 * grad
        two = 0.95 * two + 0.05 * grad * grad
        direction = one / fix_one / (jnp.sqrt(two / fix_two) + 1e-08)
        master = master - 0.00015 * (direction + 0.1 * master)
        for i, value in enumerate((master, one, two)):
            r["fresh"][i, lines] = value
        r["rounded"][lines] = master.astype(BF16)
    for h, (_, n) in enumerate(CHUNKS):
        moved = jnp.dot(r[f"select{h}"][...], r["rounded"][...], preferred_element_type=F32)
        r[f"slots{h}"][...] = moved.reshape(NDP, 4 * n, 128).astype(BF16)

        def send(i, carry, h=h):
            d = (dp + i) % NDP
            remote(
                r[f"slots{h}"].at[d],
                r[f"plane{h}"].at[dp // 4, dp % 4],
                r[f"plane_sem{h}"],
                i,
                i,
                (d, z),
            ).start()
            return carry

        lax.fori_loop(1, NDP, send, 0)
        pltpu.make_async_copy(
            r[f"slots{h}"].at[dp], r[f"plane{h}"].at[dp // 4, dp % 4], r[f"plane_sem{h}"].at[0, 0]
        ).start()
    fresh_store = pltpu.make_async_copy(r["fresh"], fresh_out, r["fresh_sem"])
    fresh_store.start()

    deep = []
    for h, (_, n) in enumerate(CHUNKS):

        def land(i, carry, h=h):
            d = (dp + NDP - i) % NDP
            remote(
                r[f"slots{h}"].at[d],
                r[f"plane{h}"].at[d // 4, d % 4],
                r[f"plane_sem{h}"],
                i,
                i,
                (d, z),
            ).wait_recv()
            return carry

        lax.fori_loop(1, NDP, land, 0)
        pltpu.make_async_copy(
            r[f"slots{h}"].at[dp], r[f"plane{h}"].at[dp // 4, dp % 4], r[f"plane_sem{h}"].at[0, 0]
        ).wait()
        there = next_out[h].at[z]
        for i in (4, 3, 5, 2, 6, 1, 7):
            to = (z + i) % DEPTH
            copy = remote(r[f"plane{h}"].at[to], there, r[f"deep_sem{h}"], i, i, (dp, to))
            copy.start()
            deep.append(copy)
        copy = pltpu.make_async_copy(r[f"plane{h}"].at[z], there, r[f"deep_sem{h}"].at[0, 0])
        copy.start()
        deep.append(copy)
    for copy in [scale_pair] + list(pair.values()) + list(first.values()) + list(second.values()):
        copy.wait_send()
    for h in range(len(CHUNKS)):

        def sent(i, carry, h=h):
            d = (dp + i) % NDP
            remote(
                r[f"slots{h}"].at[d],
                r[f"plane{h}"].at[dp // 4, dp % 4],
                r[f"plane_sem{h}"],
                i,
                i,
                (d, z),
            ).wait_send()
            return carry

        lax.fori_loop(1, NDP, sent, 0)
    for copy in [fresh_store] + deep:
        copy.wait()


def finish(fresh, *rest):
    parts = len(CHUNKS)
    arrived, outs, rows_out = rest[:parts], rest[parts : parts + 3], rest[parts + 3]
    state, state_in_sem, state_sem, rows_in_sem, rows_sem = rest[parts + 4 : parts + 9]
    rows = rest[parts + 9 :]
    loads = [pltpu.make_async_copy(fresh, state, state_in_sem)]
    loads += [pltpu.make_async_copy(arrived[h], rows[h], rows_in_sem.at[h]) for h in range(parts)]
    for copy in loads:
        copy.start()
    copies = []

    def store(src, dst, sem):
        copies.append(pltpu.make_async_copy(src, dst, sem))
        copies[-1].start()

    loads[0].wait()
    for i in range(3):
        store(state.at[i], outs[i], state_sem.at[i])
    for h, (h0, n) in enumerate(CHUNKS):
        loads[1 + h].wait()
        for m in range(DEPTH):
            store(rows[h].at[m], rows_out.at[:, pl.ds(m * TILES + h0, n)], rows_sem.at[h, m])
    for copy in copies:
        copy.wait()


def body(payload, block_scale, master, moment_one, moment_two, owner):
    def plain(array):
        return with_layout_constraint(array, Layout(tuple(range(array.ndim))))

    def fold(array, shape):
        split = array.shape[:-1] + (array.shape[-1] // 128, 128)
        return plain(jnp.swapaxes(array.reshape(split), -3, -2)).reshape(shape)

    def unfold(array):
        array = jnp.swapaxes(array, -3, -2)
        return array.reshape(array.shape[:-2] + (-1,))

    anywhere = pl.BlockSpec(memory_space=pl.ANY)
    fresh, *arrived = pl.pallas_call(
        kernel,
        out_shape=(
            jax.ShapeDtypeStruct((3, LINES, 128), F32),
            *(jax.ShapeDtypeStruct((DEPTH, 4, 4 * n, 128), BF16) for _, n in CHUNKS),
        ),
        in_specs=[anywhere] * 6,
        out_specs=(anywhere,) * (1 + len(CHUNKS)),
        scratch_shapes=list(scratch().values()),
        compiler_params=pltpu.CompilerParams(
            collective_id=0, has_side_effects=True, vmem_limit_bytes=60 * 2**20
        ),
    )(
        fold(payload[0], (SIDE, SIDE, 2, LINES, 128)),
        jnp.transpose(block_scale[0], (2, 1, 0)),
        fold(master, (LINES, 128)),
        fold(moment_one, (LINES, 128)),
        fold(moment_two, (LINES, 128)),
        owner.T,
    )
    state = jax.ShapeDtypeStruct((ROWS, TILES, 2, 128), F32)
    results = pl.pallas_call(
        finish,
        out_shape=(state, state, state, jax.ShapeDtypeStruct((8, DEPTH * TILES, 2, 128), BF16)),
        in_specs=[anywhere] * (1 + len(CHUNKS)),
        out_specs=(anywhere,) * 4,
        scratch_shapes=[
            pltpu.VMEM((3, ROWS, TILES, 2, 128), F32),
            pltpu.SemaphoreType.DMA,
            pltpu.SemaphoreType.DMA((3,)),
            pltpu.SemaphoreType.DMA((len(CHUNKS),)),
            pltpu.SemaphoreType.DMA((len(CHUNKS), DEPTH)),
            *(pltpu.VMEM((DEPTH, 8, n, 2, 128), BF16) for _, n in CHUNKS),
        ],
    )(
        fresh.reshape(3, ROWS, TILES, 2, 128),
        *(part.reshape(DEPTH, 8, n, 2, 128) for part, (_, n) in zip(arrived, CHUNKS)),
    )
    return tuple(unfold(result) for result in results)


def solution(mesh):
    return jax.shard_map(
        body,
        mesh=mesh,
        in_specs=(
            P("dp", None, None, "mp"),
            P("dp", None, None, "mp"),
            P("dp", None, "mp"),
            P("dp", None, "mp"),
            P("dp", None, "mp"),
            P("dp", None),
        ),
        out_specs=(
            P("dp", None, "mp"),
            P("dp", None, "mp"),
            P("dp", None, "mp"),
            P(("dp", "mp"), None, None),
        ),
        check_vma=False,
    )
```

```python
from types import SimpleNamespace

import jax
import jax.numpy as jnp
from jax import lax
from jax.experimental import pallas as pl
from jax.experimental.layout import Layout, with_layout_constraint
from jax.experimental.pallas import tpu as pltpu
from jax.sharding import PartitionSpec as P

STEP = 100
ROWS = 16
TILES = 10
LINES = ROWS * TILES * 2
HALF = LINES // 2
SIDE = 4
DEPTH = 8
NDP = 32
KEYS = 64
MESH = pl.DeviceIdType.MESH
BF16 = jnp.bfloat16
F32 = jnp.float32
GROUPS = (0, 1)
CHUNKS = ((0, 10),)
OFFSETS = (2, 1, 3, 0)


def iota(shape, dim):
    return lax.broadcasted_iota(jnp.int32, shape, dim)


def scratch():
    block = (HALF, 128)
    dma = pltpu.SemaphoreType.DMA

    def both(*args):
        return tuple(pltpu.VMEM(*args) for _ in GROUPS)

    return dict(
        scale=pltpu.VMEM((2, TILES, 2, 512), F32),
        keys=pltpu.VMEM((SIDE, SIDE, 2, ROWS, 2 * KEYS), F32),
        state=pltpu.VMEM((3, LINES, 128), F32),
        fresh=pltpu.VMEM((3, LINES, 128), F32),
        rounded=pltpu.VMEM((LINES, 128), BF16),
        owner=pltpu.VMEM((1, ROWS), jnp.int32),
        load_sem=dma((2, 4)),
        scale_sem=dma((4,)),
        state_sem=dma((3,)),
        fresh_sem=dma,
        known=pltpu.SemaphoreType.REGULAR((2, 3)),
        mine=both((4, SIDE) + block, BF16),
        take=both((4, SIDE) + block, BF16),
        own=both((SIDE,) + block, F32),
        first=both((3, SIDE) + block, BF16),
        relay_in=both((2, 2) + block, BF16),
        hold=both((2, 2) + block, F32),
        first_in=both((2, SIDE) + block, BF16),
        second=both((3,) + block, BF16),
        second_in=both((3,) + block, BF16),
        total=both(block, F32),
        pair_sem=tuple(dma((2, 4)) for _ in GROUPS),
        first_sem=tuple(dma((2, 6)) for _ in GROUPS),
        second_sem=tuple(dma((2, 3)) for _ in GROUPS),
        select=tuple(pltpu.VMEM((128 * n, LINES), BF16) for _, n in CHUNKS),
        slots=tuple(pltpu.VMEM((NDP, 4 * n, 128), BF16) for _, n in CHUNKS),
        plane=tuple(pltpu.VMEM((DEPTH, 4, 4 * n, 128), BF16) for _, n in CHUNKS),
        plane_sem=tuple(dma((2, NDP)) for _ in CHUNKS),
        deep_sem=tuple(dma((2, DEPTH)) for _ in CHUNKS),
    )


SCRATCH, TREE = jax.tree.flatten(scratch(), is_leaf=lambda leaf: not isinstance(leaf, (dict, tuple)))


def kernel(pay_in, scale_in, master_in, one_in, two_in, owner_in, *rest):
    fresh_out, next_out = rest[0], rest[1 : 1 + len(CHUNKS)]
    r = SimpleNamespace(**jax.tree.unflatten(TREE, rest[1 + len(CHUNKS) :]))
    dp, z = lax.axis_index("dp"), lax.axis_index("mp")
    c, y, x = dp % 2, dp // 2 % SIDE, dp // (2 * SIDE)
    centre = ((x, y), (y, x))

    def place(px, py, pc):
        return (px * SIDE + py) * 2 + pc

    def near(g, a):
        return (place(a, y, c), z) if g == 0 else (place(x, a, c), z)

    def remote(src, dst, sems, i, j, device):
        return pltpu.make_async_remote_copy(
            src, dst, sems.at[0, i], sems.at[1, j], device_id=device, device_id_type=MESH
        )

    sibling = (place(x, y, 1 - c), z)
    greeted = [sibling]
    greeted += [near(g, (centre[g][0] + i) % SIDE) for i in range(1, SIDE) for g in GROUPS]
    below, above = (dp, (z + DEPTH - 1) % DEPTH), (dp, (z + 1) % DEPTH)
    greeted += [below, above]
    barrier = pltpu.get_barrier_semaphore()
    for device in greeted:
        pl.semaphore_signal(barrier, inc=1, device_id=device, device_id_type=MESH)

    scale_load = pltpu.make_async_copy(scale_in, r.scale.at[0], r.scale_sem.at[0])
    scale_load.start()
    owner_load = pltpu.make_async_copy(owner_in, r.owner, r.scale_sem.at[1])
    owner_load.start()

    def part(g, k, core):
        a = (centre[g][0] + OFFSETS[k]) % SIDE
        lines = pl.ds(HALF * g, HALF)
        return pay_in.at[a, :, core, lines] if g == 0 else pay_in.at[:, a, core, lines]

    loads = {
        (g, k): pltpu.make_async_copy(part(g, k, c), r.mine[g].at[k], r.load_sem.at[g, k])
        for k in range(4)
        for g in GROUPS
    }
    state_loads = [
        pltpu.make_async_copy(ref, r.state.at[i], r.state_sem.at[i])
        for i, ref in enumerate((master_in, one_in, two_in))
    ]
    for copy in list(loads.values()) + state_loads:
        copy.start()
    pl.semaphore_wait(barrier, len(greeted))

    scale_pair = pltpu.make_async_remote_copy(
        scale_in,
        r.scale.at[1],
        r.scale_sem.at[2],
        r.scale_sem.at[3],
        device_id=sibling,
        device_id_type=MESH,
    )
    scale_pair.start()
    pair = {}
    for k in range(4):
        for g in GROUPS:
            pair[g, k] = remote(
                part(g, k, 1 - c), r.take[g].at[k], r.pair_sem[g], k, k, sibling
            )
            pair[g, k].start()

    def tell(step):
        for way, device in ((0, above), (1, below)):
            if (way, step) != (0, 2):
                pl.semaphore_signal(
                    r.known.at[way, step], inc=1, device_id=device, device_id_type=MESH
                )

    def learn(step):
        for way in range(2):
            if (way, step) != (0, 2):
                pl.semaphore_wait(r.known.at[way, step], 1)

    tell(0)

    scale_load.wait()
    scale_pair.wait_recv()
    eye = (iota((128, 128), 0) == iota((128, 128), 1)).astype(BF16)
    for k in range(4):
        parts = []
        for core in range(2):
            whole = [r.scale[core, :, i, 128 * k : 128 * k + 128] for i in range(2)]
            for _ in range(3):
                near_by = [value.astype(BF16).astype(F32) for value in whole]
                whole = [value - close for value, close in zip(whole, near_by)]
                parts += near_by
            parts.append(jnp.zeros((KEYS - 60, 128), F32))
        turned = lax.dot_general(
            eye,
            jnp.concatenate(parts, axis=0).astype(BF16),
            (((1,), (1,)), ((), ())),
            preferred_element_type=F32,
        )
        r.keys[k] = turned.reshape(4, 2, ROWS, 2 * KEYS)

    unit = SIDE * HALF
    repeat = (iota((unit, 32), 0) // (2 * TILES) == iota((unit, 32), 1)).astype(BF16)
    line = iota((unit, 2 * KEYS), 0) % (2 * TILES)
    match = iota((unit, 2 * KEYS), 1) % KEYS % (2 * TILES) == line % 2 * TILES + line // 2
    ones = (iota((2 * KEYS, 256), 0) // KEYS == iota((2 * KEYS, 256), 1) // 128).astype(BF16)

    def terms(g, k):
        a = (centre[g][0] + OFFSETS[k]) % SIDE
        rows = slice(8 * g, 8 * g + 8)
        keys = r.keys[a, :, c, rows] if g == 0 else r.keys[:, a, c, rows]
        many = jnp.dot(repeat, keys.reshape(32, 2 * KEYS).astype(BF16), preferred_element_type=F32)
        many = jnp.where(match, many, 0.0).astype(BF16)
        scales = jnp.dot(many, ones, preferred_element_type=F32)
        loads[g, k].wait()
        pair[g, k].wait_recv()
        total = r.mine[g][k].astype(F32).reshape(unit, 128) * scales[:, :128]
        total += r.take[g][k].astype(F32).reshape(unit, 128) * scales[:, 128:]
        return total.reshape(SIDE, HALF, 128)

    first = {}
    lower, upper = slice(0, 2), slice(2, 4)

    def pass_on(g, number, source, target, step):
        first[g, number] = remote(
            source,
            target,
            r.first_sem[g],
            number,
            number,
            near(g, (centre[g][0] + step) % SIDE),
        )
        first[g, number].start()

    for g in GROUPS:
        r.first[g][0] = terms(g, 0).astype(BF16)
        sent_ref, relay = r.first[g].at[0], r.relay_in[g]
        pass_on(g, 0, sent_ref.at[pl.ds(0, 2)], relay.at[0], 1)
        pass_on(g, 1, sent_ref.at[pl.ds(2, 2)], relay.at[1], 3)
    for side, (k, step, now, later, start) in enumerate(
        ((1, 1, upper, lower, 2), (2, 3, lower, upper, 0))
    ):
        for g in GROUPS:
            total = terms(g, k)
            r.first[g][k, now] = total[now].astype(BF16)
            pass_on(
                g,
                2 + 2 * side,
                r.first[g].at[k, pl.ds(start, 2)],
                r.first_in[g].at[side, pl.ds(start, 2)],
                step,
            )
            r.hold[g][side] = total[later]
    for side, (k, step, later, start) in enumerate(((1, 1, lower, 0), (2, 3, upper, 2))):
        for g in GROUPS:
            first[g, side].wait_recv()
            r.first[g][k, later] = (
                r.hold[g][side] + r.relay_in[g][side].astype(F32)
            ).astype(BF16)
            pass_on(
                g,
                3 + 2 * side,
                r.first[g].at[k, pl.ds(start, 2)],
                r.first_in[g].at[side, pl.ds(start, 2)],
                step,
            )
    for g in GROUPS:
        r.own[g][...] = terms(g, 3)
    learn(0)
    tell(1)

    owner_load.wait()
    targets = r.owner[...].astype(F32)
    square = (ROWS, ROWS)
    diagonal = jnp.where(iota(square, 0) == iota(square, 1), jnp.broadcast_to(targets, square), 0.0)
    columns = jnp.dot(diagonal.astype(BF16), jnp.ones(square, BF16), preferred_element_type=F32)
    earlier = (columns == targets) & (iota(square, 0) < iota(square, 1))
    rank = jnp.sum(jnp.where(earlier, 1.0, 0.0), axis=0, keepdims=True)
    slot = jnp.broadcast_to(targets * 2.0 + rank, (8, ROWS)).astype(BF16)
    wide = (ROWS, LINES)
    stretch = (iota(wide, 1) // (2 * TILES) == iota(wide, 0)).astype(BF16)
    slot = jnp.dot(slot, stretch, preferred_element_type=F32)[0:1].astype(jnp.int32)
    line = iota((1, LINES), 1) % (2 * TILES)
    for h, (h0, n) in enumerate(CHUNKS):
        inside = (line >= 2 * h0) & (line < 2 * h0 + 2 * n)
        goal = jnp.where(inside, slot * (2 * n) + line - 2 * h0, -1)
        r.select[h][...] = (iota((128 * n, LINES), 0) == goal).astype(BF16)
    for copy in state_loads:
        copy.wait()

    learn(1)
    tell(2)

    second = {}
    for g in GROUPS:
        b0 = centre[g][1]
        for number in range(2, 6):
            first[g, number].wait_recv()
        for k in range(4):
            b = (b0 + OFFSETS[k]) % SIDE
            total = r.own[g][b]
            for j in range(2):
                total += r.first_in[g][j, b].astype(F32)
            if k == 3:
                r.total[g][...] = total
                continue
            r.second[g][k] = total.astype(BF16)
            second[g, k] = remote(
                r.second[g].at[k],
                r.second_in[g].at[k],
                r.second_sem[g],
                k,
                k,
                near(1 - g, b),
            )
            second[g, k].start()

    fix_one = 1.0 - 0.9 ** (STEP + 1)
    fix_two = 1.0 - 0.95 ** (STEP + 1)
    for g in GROUPS:
        for k in range(3):
            second[g, k].wait_recv()
        lines = slice(HALF * g, HALF * g + HALF)
        grad = r.total[g][...]
        for j in range(3):
            grad += r.second_in[g][j].astype(F32)
        master, one, two = (r.state[i, lines] for i in range(3))
        one = 0.9 * one + 0.1 * grad
        two = 0.95 * two + 0.05 * grad * grad
        direction = one / fix_one / (jnp.sqrt(two / fix_two) + 1e-08)
        master = master - 0.00015 * (direction + 0.1 * master)
        for i, value in enumerate((master, one, two)):
            r.fresh[i, lines] = value
        r.rounded[lines] = master.astype(BF16)
    for h, (_, n) in enumerate(CHUNKS):
        moved = jnp.dot(r.select[h][...], r.rounded[...], preferred_element_type=F32)
        r.slots[h][...] = moved.reshape(NDP, 4 * n, 128).astype(BF16)

        def send(i, carry, h=h):
            d = (dp + i) % NDP
            remote(
                r.slots[h].at[d],
                r.plane[h].at[dp // 4, dp % 4],
                r.plane_sem[h],
                i,
                i,
                (d, z),
            ).start()
            return carry

        lax.fori_loop(1, NDP, send, 0)
        pltpu.make_async_copy(
            r.slots[h].at[dp], r.plane[h].at[dp // 4, dp % 4], r.plane_sem[h].at[0, 0]
        ).start()
    fresh_store = pltpu.make_async_copy(r.fresh, fresh_out, r.fresh_sem)
    fresh_store.start()

    learn(2)
    deep = []
    for h, (_, n) in enumerate(CHUNKS):

        def land(i, carry, h=h):
            d = (dp + NDP - i) % NDP
            remote(
                r.slots[h].at[d],
                r.plane[h].at[d // 4, d % 4],
                r.plane_sem[h],
                i,
                i,
                (d, z),
            ).wait_recv()
            return carry

        lax.fori_loop(1, NDP, land, 0)
        pltpu.make_async_copy(
            r.slots[h].at[dp], r.plane[h].at[dp // 4, dp % 4], r.plane_sem[h].at[0, 0]
        ).wait()
        there = next_out[h].at[z]
        for i in (4, 3, 5, 2, 6, 1, 7):
            to = (z + i) % DEPTH
            copy = remote(r.plane[h].at[to], there, r.deep_sem[h], i, i, (dp, to))
            copy.start()
            deep.append(copy)
        copy = pltpu.make_async_copy(r.plane[h].at[z], there, r.deep_sem[h].at[0, 0])
        copy.start()
        deep.append(copy)
    for copy in [scale_pair] + list(pair.values()) + list(first.values()) + list(second.values()):
        copy.wait_send()
    for h in range(len(CHUNKS)):

        def sent(i, carry, h=h):
            d = (dp + i) % NDP
            remote(
                r.slots[h].at[d],
                r.plane[h].at[dp // 4, dp % 4],
                r.plane_sem[h],
                i,
                i,
                (d, z),
            ).wait_send()
            return carry

        lax.fori_loop(1, NDP, sent, 0)
    for copy in [fresh_store] + deep:
        copy.wait()


def finish(fresh, *rest):
    parts = len(CHUNKS)
    arrived, outs, rows_out = rest[:parts], rest[parts : parts + 3], rest[parts + 3]
    state, state_in_sem, state_sem, rows_in_sem, rows_sem = rest[parts + 4 : parts + 9]
    rows = rest[parts + 9 :]
    loads = [pltpu.make_async_copy(fresh, state, state_in_sem)]
    loads += [pltpu.make_async_copy(arrived[h], rows[h], rows_in_sem.at[h]) for h in range(parts)]
    for copy in loads:
        copy.start()
    copies = []

    def store(src, dst, sem):
        copies.append(pltpu.make_async_copy(src, dst, sem))
        copies[-1].start()

    loads[0].wait()
    for i in range(3):
        store(state.at[i], outs[i], state_sem.at[i])
    for h, (h0, n) in enumerate(CHUNKS):
        loads[1 + h].wait()
        for m in range(DEPTH):
            store(rows[h].at[m], rows_out.at[:, pl.ds(m * TILES + h0, n)], rows_sem.at[h, m])
    for copy in copies:
        copy.wait()


def body(payload, block_scale, master, moment_one, moment_two, owner):
    def plain(array):
        return with_layout_constraint(array, Layout(tuple(range(array.ndim))))

    def fold(array, shape):
        split = array.shape[:-1] + (array.shape[-1] // 128, 128)
        return plain(jnp.swapaxes(array.reshape(split), -3, -2)).reshape(shape)

    def unfold(array):
        array = jnp.swapaxes(array, -3, -2)
        return array.reshape(array.shape[:-2] + (-1,))

    anywhere = pl.BlockSpec(memory_space=pl.ANY)
    fresh, *arrived = pl.pallas_call(
        kernel,
        out_shape=(
            jax.ShapeDtypeStruct((3, LINES, 128), F32),
            *(jax.ShapeDtypeStruct((DEPTH, 4, 4 * n, 128), BF16) for _, n in CHUNKS),
        ),
        in_specs=[anywhere] * 6,
        out_specs=(anywhere,) * (1 + len(CHUNKS)),
        scratch_shapes=SCRATCH,
        compiler_params=pltpu.CompilerParams(
            collective_id=0, has_side_effects=True, vmem_limit_bytes=60 * 2**20
        ),
    )(
        fold(payload[0], (SIDE, SIDE, 2, LINES, 128)),
        jnp.transpose(block_scale[0], (2, 1, 0)),
        fold(master, (LINES, 128)),
        fold(moment_one, (LINES, 128)),
        fold(moment_two, (LINES, 128)),
        owner.T,
    )
    state = jax.ShapeDtypeStruct((ROWS, TILES, 2, 128), F32)
    results = pl.pallas_call(
        finish,
        out_shape=(state, state, state, jax.ShapeDtypeStruct((8, DEPTH * TILES, 2, 128), BF16)),
        in_specs=[anywhere] * (1 + len(CHUNKS)),
        out_specs=(anywhere,) * 4,
        scratch_shapes=[
            pltpu.VMEM((3, ROWS, TILES, 2, 128), F32),
            pltpu.SemaphoreType.DMA,
            pltpu.SemaphoreType.DMA((3,)),
            pltpu.SemaphoreType.DMA((len(CHUNKS),)),
            pltpu.SemaphoreType.DMA((len(CHUNKS), DEPTH)),
            *(pltpu.VMEM((DEPTH, 8, n, 2, 128), BF16) for _, n in CHUNKS),
        ],
    )(
        fresh.reshape(3, ROWS, TILES, 2, 128),
        *(part.reshape(DEPTH, 8, n, 2, 128) for part, (_, n) in zip(arrived, CHUNKS)),
    )
    return tuple(unfold(result) for result in results)


def solution(mesh):
    return jax.shard_map(
        body,
        mesh=mesh,
        in_specs=(
            P("dp", None, None, "mp"),
            P("dp", None, None, "mp"),
            P("dp", None, "mp"),
            P("dp", None, "mp"),
            P("dp", None, "mp"),
            P("dp", None),
        ),
        out_specs=(
            P("dp", None, "mp"),
            P("dp", None, "mp"),
            P("dp", None, "mp"),
            P(("dp", "mp"), None, None),
        ),
        check_vma=False,
    )
```

```python
from types import SimpleNamespace

import jax
import jax.numpy as jnp
from jax import lax
from jax.experimental import pallas as pl
from jax.experimental.layout import Layout, with_layout_constraint
from jax.experimental.pallas import tpu as pltpu
from jax.sharding import PartitionSpec as P

STEP = 100
ROWS = 16
TILES = 10
LINES = ROWS * TILES * 2
HALF = LINES // 2
SIDE = 4
DEPTH = 8
NDP = 32
KEYS = 64
MESH = pl.DeviceIdType.MESH
BF16 = jnp.bfloat16
F32 = jnp.float32
GROUPS = (0, 1)
CHUNKS = ((0, 10),)
OFFSETS = (2, 1, 3, 0)
AWAY = sorted(
    ((i, j, core) for i in range(SIDE) for j in range(SIDE) for core in range(2) if (i, j, core) != (0, 0, 0)),
    key=lambda step: -min(step[0], SIDE - step[0]) - min(step[1], SIDE - step[1]),
)


def iota(shape, dim):
    return lax.broadcasted_iota(jnp.int32, shape, dim)


def scratch():
    block = (HALF, 128)
    dma = pltpu.SemaphoreType.DMA

    def both(*args):
        return tuple(pltpu.VMEM(*args) for _ in GROUPS)

    return dict(
        scale=pltpu.VMEM((2, TILES, 2, 512), F32),
        keys=pltpu.VMEM((SIDE, SIDE, 2, ROWS, 2 * KEYS), F32),
        state=pltpu.VMEM((3, LINES, 128), F32),
        fresh=pltpu.VMEM((3, LINES, 128), F32),
        rounded=pltpu.VMEM((LINES, 128), BF16),
        owner=pltpu.VMEM((1, ROWS), jnp.int32),
        load_sem=dma((2, 4)),
        scale_sem=dma((4,)),
        state_sem=dma((3,)),
        fresh_sem=dma,
        known=pltpu.SemaphoreType.REGULAR((2, 3)),
        mine=both((4, SIDE) + block, BF16),
        take=both((4, SIDE) + block, BF16),
        own=both((SIDE,) + block, F32),
        first=both((3, SIDE) + block, BF16),
        relay_in=both((2, 2) + block, BF16),
        hold=both((2, 2) + block, F32),
        first_in=both((2, SIDE) + block, BF16),
        second=both((3,) + block, BF16),
        second_in=both((3,) + block, BF16),
        total=both(block, F32),
        pair_sem=tuple(dma((2, 4)) for _ in GROUPS),
        first_sem=tuple(dma((2, 6)) for _ in GROUPS),
        second_sem=tuple(dma((2, 3)) for _ in GROUPS),
        select=tuple(pltpu.VMEM((128 * n, LINES), BF16) for _, n in CHUNKS),
        slots=tuple(pltpu.VMEM((NDP, 4 * n, 128), BF16) for _, n in CHUNKS),
        plane=tuple(pltpu.VMEM((DEPTH, 4, 4 * n, 128), BF16) for _, n in CHUNKS),
        plane_sem=tuple(dma((2, NDP)) for _ in CHUNKS),
        deep_sem=tuple(dma((2, DEPTH)) for _ in CHUNKS),
    )


SCRATCH, TREE = jax.tree.flatten(scratch(), is_leaf=lambda leaf: not isinstance(leaf, (dict, tuple)))


def kernel(pay_in, scale_in, master_in, one_in, two_in, owner_in, *rest):
    fresh_out, next_out = rest[0], rest[1 : 1 + len(CHUNKS)]
    r = SimpleNamespace(**jax.tree.unflatten(TREE, rest[1 + len(CHUNKS) :]))
    dp, z = lax.axis_index("dp"), lax.axis_index("mp")
    c, y, x = dp % 2, dp // 2 % SIDE, dp // (2 * SIDE)
    centre = ((x, y), (y, x))

    def place(px, py, pc):
        return (px * SIDE + py) * 2 + pc

    def near(g, a):
        return (place(a, y, c), z) if g == 0 else (place(x, a, c), z)

    def remote(src, dst, sems, i, j, device):
        return pltpu.make_async_remote_copy(
            src, dst, sems.at[0, i], sems.at[1, j], device_id=device, device_id_type=MESH
        )

    sibling = (place(x, y, 1 - c), z)
    greeted = [sibling]
    greeted += [near(g, (centre[g][0] + i) % SIDE) for i in range(1, SIDE) for g in GROUPS]
    below, above = (dp, (z + DEPTH - 1) % DEPTH), (dp, (z + 1) % DEPTH)
    greeted += [below, above]
    barrier = pltpu.get_barrier_semaphore()
    for device in greeted:
        pl.semaphore_signal(barrier, inc=1, device_id=device, device_id_type=MESH)

    scale_load = pltpu.make_async_copy(scale_in, r.scale.at[0], r.scale_sem.at[0])
    scale_load.start()
    owner_load = pltpu.make_async_copy(owner_in, r.owner, r.scale_sem.at[1])
    owner_load.start()

    def part(g, k, core):
        a = (centre[g][0] + OFFSETS[k]) % SIDE
        lines = pl.ds(HALF * g, HALF)
        return pay_in.at[a, :, core, lines] if g == 0 else pay_in.at[:, a, core, lines]

    loads = {
        (g, k): pltpu.make_async_copy(part(g, k, c), r.mine[g].at[k], r.load_sem.at[g, k])
        for k in range(4)
        for g in GROUPS
    }
    state_loads = [
        pltpu.make_async_copy(ref, r.state.at[i], r.state_sem.at[i])
        for i, ref in enumerate((master_in, one_in, two_in))
    ]
    for copy in list(loads.values()) + state_loads:
        copy.start()
    pl.semaphore_wait(barrier, len(greeted))

    scale_pair = pltpu.make_async_remote_copy(
        scale_in,
        r.scale.at[1],
        r.scale_sem.at[2],
        r.scale_sem.at[3],
        device_id=sibling,
        device_id_type=MESH,
    )
    scale_pair.start()
    pair = {}
    for k in range(4):
        for g in GROUPS:
            pair[g, k] = remote(
                part(g, k, 1 - c), r.take[g].at[k], r.pair_sem[g], k, k, sibling
            )
    for g in GROUPS:
        pair[g, 0].start()

    def tell(step):
        for way, device in ((0, above), (1, below)):
            if (way, step) != (0, 2):
                pl.semaphore_signal(
                    r.known.at[way, step], inc=1, device_id=device, device_id_type=MESH
                )

    def learn(step):
        for way in range(2):
            if (way, step) != (0, 2):
                pl.semaphore_wait(r.known.at[way, step], 1)

    tell(0)

    scale_load.wait()
    scale_pair.wait_recv()
    for k in range(1, 4):
        for g in GROUPS:
            pair[g, k].start()
    eye = (iota((128, 128), 0) == iota((128, 128), 1)).astype(BF16)
    for k in range(4):
        parts = []
        for core in range(2):
            whole = [r.scale[core, :, i, 128 * k : 128 * k + 128] for i in range(2)]
            for _ in range(3):
                near_by = [value.astype(BF16).astype(F32) for value in whole]
                whole = [value - close for value, close in zip(whole, near_by)]
                parts += near_by
            parts.append(jnp.zeros((KEYS - 60, 128), F32))
        turned = lax.dot_general(
            eye,
            jnp.concatenate(parts, axis=0).astype(BF16),
            (((1,), (1,)), ((), ())),
            preferred_element_type=F32,
        )
        r.keys[k] = turned.reshape(4, 2, ROWS, 2 * KEYS)

    unit = SIDE * HALF
    repeat = (iota((unit, 32), 0) // (2 * TILES) == iota((unit, 32), 1)).astype(BF16)
    line = iota((unit, 2 * KEYS), 0) % (2 * TILES)
    match = iota((unit, 2 * KEYS), 1) % KEYS % (2 * TILES) == line % 2 * TILES + line // 2
    ones = (iota((2 * KEYS, 256), 0) // KEYS == iota((2 * KEYS, 256), 1) // 128).astype(BF16)

    def terms(g, k):
        a = (centre[g][0] + OFFSETS[k]) % SIDE
        rows = slice(8 * g, 8 * g + 8)
        keys = r.keys[a, :, c, rows] if g == 0 else r.keys[:, a, c, rows]
        many = jnp.dot(repeat, keys.reshape(32, 2 * KEYS).astype(BF16), preferred_element_type=F32)
        many = jnp.where(match, many, 0.0).astype(BF16)
        scales = jnp.dot(many, ones, preferred_element_type=F32)
        loads[g, k].wait()
        pair[g, k].wait_recv()
        total = r.mine[g][k].astype(F32).reshape(unit, 128) * scales[:, :128]
        total += r.take[g][k].astype(F32).reshape(unit, 128) * scales[:, 128:]
        return total.reshape(SIDE, HALF, 128)

    first = {}
    lower, upper = slice(0, 2), slice(2, 4)

    def pass_on(g, number, source, target, step):
        first[g, number] = remote(
            source,
            target,
            r.first_sem[g],
            number,
            number,
            near(g, (centre[g][0] + step) % SIDE),
        )
        first[g, number].start()

    for g in GROUPS:
        r.first[g][0] = terms(g, 0).astype(BF16)
        sent_ref, relay = r.first[g].at[0], r.relay_in[g]
        pass_on(g, 0, sent_ref.at[pl.ds(0, 2)], relay.at[0], 1)
        pass_on(g, 1, sent_ref.at[pl.ds(2, 2)], relay.at[1], 3)
    for side, (k, step, now, later, start) in enumerate(
        ((1, 1, upper, lower, 2), (2, 3, lower, upper, 0))
    ):
        for g in GROUPS:
            total = terms(g, k)
            r.first[g][k, now] = total[now].astype(BF16)
            pass_on(
                g,
                2 + 2 * side,
                r.first[g].at[k, pl.ds(start, 2)],
                r.first_in[g].at[side, pl.ds(start, 2)],
                step,
            )
            r.hold[g][side] = total[later]
    for side, (k, step, later, start) in enumerate(((1, 1, lower, 0), (2, 3, upper, 2))):
        for g in GROUPS:
            first[g, side].wait_recv()
            r.first[g][k, later] = (
                r.hold[g][side] + r.relay_in[g][side].astype(F32)
            ).astype(BF16)
            pass_on(
                g,
                3 + 2 * side,
                r.first[g].at[k, pl.ds(start, 2)],
                r.first_in[g].at[side, pl.ds(start, 2)],
                step,
            )
    for g in GROUPS:
        r.own[g][...] = terms(g, 3)
    learn(0)
    tell(1)

    owner_load.wait()
    targets = r.owner[...].astype(F32)
    square = (ROWS, ROWS)
    diagonal = jnp.where(iota(square, 0) == iota(square, 1), jnp.broadcast_to(targets, square), 0.0)
    columns = jnp.dot(diagonal.astype(BF16), jnp.ones(square, BF16), preferred_element_type=F32)
    earlier = (columns == targets) & (iota(square, 0) < iota(square, 1))
    rank = jnp.sum(jnp.where(earlier, 1.0, 0.0), axis=0, keepdims=True)
    slot = jnp.broadcast_to(targets * 2.0 + rank, (8, ROWS)).astype(BF16)
    wide = (ROWS, LINES)
    stretch = (iota(wide, 1) // (2 * TILES) == iota(wide, 0)).astype(BF16)
    slot = jnp.dot(slot, stretch, preferred_element_type=F32)[0:1].astype(jnp.int32)
    line = iota((1, LINES), 1) % (2 * TILES)
    for h, (h0, n) in enumerate(CHUNKS):
        inside = (line >= 2 * h0) & (line < 2 * h0 + 2 * n)
        goal = jnp.where(inside, slot * (2 * n) + line - 2 * h0, -1)
        r.select[h][...] = (iota((128 * n, LINES), 0) == goal).astype(BF16)
    for copy in state_loads:
        copy.wait()

    learn(1)
    tell(2)

    second = {}
    for g in GROUPS:
        b0 = centre[g][1]
        for number in range(2, 6):
            first[g, number].wait_recv()
        for k in range(4):
            b = (b0 + OFFSETS[k]) % SIDE
            total = r.own[g][b]
            for j in range(2):
                total += r.first_in[g][j, b].astype(F32)
            if k == 3:
                r.total[g][...] = total
                continue
            r.second[g][k] = total.astype(BF16)
            second[g, k] = remote(
                r.second[g].at[k],
                r.second_in[g].at[k],
                r.second_sem[g],
                k,
                k,
                near(1 - g, b),
            )
            second[g, k].start()

    fix_one = 1.0 - 0.9 ** (STEP + 1)
    fix_two = 1.0 - 0.95 ** (STEP + 1)
    for g in GROUPS:
        for k in range(3):
            second[g, k].wait_recv()
        lines = slice(HALF * g, HALF * g + HALF)
        grad = r.total[g][...]
        for j in range(3):
            grad += r.second_in[g][j].astype(F32)
        master, one, two = (r.state[i, lines] for i in range(3))
        one = 0.9 * one + 0.1 * grad
        two = 0.95 * two + 0.05 * grad * grad
        direction = one / fix_one / (jnp.sqrt(two / fix_two) + 1e-08)
        master = master - 0.00015 * (direction + 0.1 * master)
        for i, value in enumerate((master, one, two)):
            r.fresh[i, lines] = value
        r.rounded[lines] = master.astype(BF16)
    spread = []
    for h, (_, n) in enumerate(CHUNKS):
        moved = jnp.dot(r.select[h][...], r.rounded[...], preferred_element_type=F32)
        r.slots[h][...] = moved.reshape(NDP, 4 * n, 128).astype(BF16)

        for i, j, core in AWAY:
            d = place((x + i) % SIDE, (y + j) % SIDE, (c + core) % 2)
            copy = remote(
                r.slots[h].at[d],
                r.plane[h].at[dp // 4, dp % 4],
                r.plane_sem[h],
                place(i, j, core),
                place(i, j, core),
                (d, z),
            )
            copy.start()
            spread.append(copy)
        pltpu.make_async_copy(
            r.slots[h].at[dp], r.plane[h].at[dp // 4, dp % 4], r.plane_sem[h].at[1, 0]
        ).start()
    fresh_store = pltpu.make_async_copy(r.fresh, fresh_out, r.fresh_sem)
    fresh_store.start()

    learn(2)
    deep = []

    def arrive(h, to):
        for i in range(4):
            source = 4 * to + i
            away = place(
                (x + SIDE - source // 8) % SIDE, (y + SIDE - source // 2 % SIDE) % SIDE, (c + source) % 2
            )
            slots = r.plane[h].at[to, i]
            pltpu.make_async_copy(slots, slots, r.plane_sem[h].at[1, away]).wait()

    for h, (_, n) in enumerate(CHUNKS):

        there = next_out[h].at[z]
        for i in (4, 3, 5, 2, 6, 1, 7):
            to = (z + i) % DEPTH
            arrive(h, to)
            copy = remote(r.plane[h].at[to], there, r.deep_sem[h], i, i, (dp, to))
            copy.start()
            deep.append(copy)
        arrive(h, z)
        copy = pltpu.make_async_copy(r.plane[h].at[z], there, r.deep_sem[h].at[0, 0])
        copy.start()
        deep.append(copy)
    for copy in [scale_pair] + list(pair.values()) + list(first.values()) + list(second.values()):
        copy.wait_send()
    for copy in spread:
        copy.wait_send()
    for copy in [fresh_store] + deep:
        copy.wait()


def finish(fresh, *rest):
    parts = len(CHUNKS)
    arrived, outs, rows_out = rest[:parts], rest[parts : parts + 3], rest[parts + 3]
    state_sem, rows_sem = rest[parts + 4 :]
    copies = [
        pltpu.make_async_copy(
            arrived[h].at[m], rows_out.at[:, pl.ds(m * TILES + h0, n)], rows_sem.at[h, m]
        )
        for h, (h0, n) in enumerate(CHUNKS)
        for m in range(DEPTH)
    ]
    copies += [pltpu.make_async_copy(fresh.at[i], outs[i], state_sem.at[i]) for i in range(3)]
    for copy in copies:
        copy.start()
    for copy in copies:
        copy.wait()


def body(payload, block_scale, master, moment_one, moment_two, owner):
    def plain(array):
        return with_layout_constraint(array, Layout(tuple(range(array.ndim))))

    def fold(array, shape):
        split = array.shape[:-1] + (array.shape[-1] // 128, 128)
        return plain(jnp.swapaxes(array.reshape(split), -3, -2)).reshape(shape)

    def unfold(array):
        array = jnp.swapaxes(array, -3, -2)
        return array.reshape(array.shape[:-2] + (-1,))

    anywhere = pl.BlockSpec(memory_space=pl.ANY)
    fresh, *arrived = pl.pallas_call(
        kernel,
        out_shape=(
            jax.ShapeDtypeStruct((3, LINES, 128), F32),
            *(jax.ShapeDtypeStruct((DEPTH, 4, 4 * n, 128), BF16) for _, n in CHUNKS),
        ),
        in_specs=[anywhere] * 6,
        out_specs=(anywhere,) * (1 + len(CHUNKS)),
        scratch_shapes=SCRATCH,
        compiler_params=pltpu.CompilerParams(
            collective_id=0, has_side_effects=True, vmem_limit_bytes=52 * 2**20
        ),
    )(
        *(pltpu.with_memory_space_constraint(array, pltpu.HBM) for array in (
        fold(payload[0], (SIDE, SIDE, 2, LINES, 128)),
        jnp.transpose(block_scale[0], (2, 1, 0)),
        fold(master, (LINES, 128)),
        fold(moment_one, (LINES, 128)),
        fold(moment_two, (LINES, 128)),
        owner.T,
        ))
    )
    state = jax.ShapeDtypeStruct((ROWS, TILES, 2, 128), F32)
    results = pl.pallas_call(
        finish,
        out_shape=(state, state, state, jax.ShapeDtypeStruct((8, DEPTH * TILES, 2, 128), BF16)),
        in_specs=[anywhere] * (1 + len(CHUNKS)),
        out_specs=(anywhere,) * 4,
        scratch_shapes=[
            pltpu.SemaphoreType.DMA((3,)),
            pltpu.SemaphoreType.DMA((len(CHUNKS), DEPTH)),
        ],
        compiler_params=pltpu.CompilerParams(vmem_limit_bytes=8 * 2**20),
    )(
        fresh.reshape(3, ROWS, TILES, 2, 128),
        *(part.reshape(DEPTH, 8, n, 2, 128) for part, (_, n) in zip(arrived, CHUNKS)),
    )
    return tuple(unfold(result) for result in results)


def solution(mesh):
    return jax.shard_map(
        body,
        mesh=mesh,
        in_specs=(
            P("dp", None, None, "mp"),
            P("dp", None, None, "mp"),
            P("dp", None, "mp"),
            P("dp", None, "mp"),
            P("dp", None, "mp"),
            P("dp", None),
        ),
        out_specs=(
            P("dp", None, "mp"),
            P("dp", None, "mp"),
            P("dp", None, "mp"),
            P(("dp", "mp"), None, None),
        ),
        check_vma=False,
    )
```

```python
from types import SimpleNamespace

import jax
import jax.numpy as jnp
from jax import lax
from jax.experimental import pallas as pl
from jax.experimental.layout import Layout, with_layout_constraint
from jax.experimental.pallas import tpu as pltpu
from jax.sharding import PartitionSpec as P

STEP = 100
ROWS = 16
TILES = 10
LINES = ROWS * TILES * 2
HALF = LINES // 2
SIDE = 4
DEPTH = 8
NDP = 32
KEYS = 64
MESH = pl.DeviceIdType.MESH
BF16 = jnp.bfloat16
F32 = jnp.float32
GROUPS = (0, 1)
CHUNKS = ((0, 4), (4, 6))
OFFSETS = (2, 1, 3, 0)
AWAY = sorted(
    ((i, j, core) for i in range(SIDE) for j in range(SIDE) for core in range(2) if (i, j, core) != (0, 0, 0)),
    key=lambda step: -min(step[0], SIDE - step[0]) - min(step[1], SIDE - step[1]),
)


def iota(shape, dim):
    return lax.broadcasted_iota(jnp.int32, shape, dim)


def scratch():
    block = (HALF, 128)
    dma = pltpu.SemaphoreType.DMA

    def both(*args):
        return tuple(pltpu.VMEM(*args) for _ in GROUPS)

    return dict(
        scale=pltpu.VMEM((2, TILES, 2, 512), F32),
        keys=pltpu.VMEM((SIDE, SIDE, 2, ROWS, 2 * KEYS), F32),
        state=pltpu.VMEM((3, LINES, 128), F32),
        fresh=pltpu.VMEM((3, LINES, 128), F32),
        rounded=pltpu.VMEM((LINES, 128), BF16),
        owner=pltpu.VMEM((1, ROWS), jnp.int32),
        load_sem=dma((2, 4)),
        scale_sem=dma((4,)),
        state_sem=dma((3,)),
        fresh_sem=dma,
        known=pltpu.SemaphoreType.REGULAR((2, 3)),
        mine=both((4, SIDE) + block, BF16),
        take=both((4, SIDE) + block, BF16),
        own=both((SIDE,) + block, F32),
        first=both((3, SIDE) + block, BF16),
        relay_in=both((2, 2) + block, BF16),
        hold=both((2, 2) + block, F32),
        first_in=both((2, SIDE) + block, BF16),
        second=both((3,) + block, BF16),
        second_in=both((3,) + block, BF16),
        total=both(block, F32),
        pair_sem=tuple(dma((2, 4)) for _ in GROUPS),
        first_sem=tuple(dma((2, 6)) for _ in GROUPS),
        second_sem=tuple(dma((2, 3)) for _ in GROUPS),
        select=tuple(pltpu.VMEM((128 * n, LINES), BF16) for _, n in CHUNKS),
        slots=tuple(pltpu.VMEM((NDP, 4 * n, 128), BF16) for _, n in CHUNKS),
        plane=tuple(pltpu.VMEM((DEPTH, 4, 4 * n, 128), BF16) for _, n in CHUNKS),
        plane_sem=tuple(dma((2, NDP)) for _ in CHUNKS),
        deep_sem=tuple(dma((2, DEPTH)) for _ in CHUNKS),
    )


SCRATCH, TREE = jax.tree.flatten(scratch(), is_leaf=lambda leaf: not isinstance(leaf, (dict, tuple)))


def kernel(pay_in, scale_in, master_in, one_in, two_in, owner_in, *rest):
    fresh_out, next_out = rest[0], rest[1 : 1 + len(CHUNKS)]
    r = SimpleNamespace(**jax.tree.unflatten(TREE, rest[1 + len(CHUNKS) :]))
    dp, z = lax.axis_index("dp"), lax.axis_index("mp")
    c, y, x = dp % 2, dp // 2 % SIDE, dp // (2 * SIDE)
    centre = ((x, y), (y, x))

    def place(px, py, pc):
        return (px * SIDE + py) * 2 + pc

    def near(g, a):
        return (place(a, y, c), z) if g == 0 else (place(x, a, c), z)

    def remote(src, dst, sems, i, j, device):
        return pltpu.make_async_remote_copy(
            src, dst, sems.at[0, i], sems.at[1, j], device_id=device, device_id_type=MESH
        )

    sibling = (place(x, y, 1 - c), z)
    greeted = [sibling]
    greeted += [near(g, (centre[g][0] + i) % SIDE) for i in range(1, SIDE) for g in GROUPS]
    below, above = (dp, (z + DEPTH - 1) % DEPTH), (dp, (z + 1) % DEPTH)
    greeted += [below, above]
    barrier = pltpu.get_barrier_semaphore()
    for device in greeted:
        pl.semaphore_signal(barrier, inc=1, device_id=device, device_id_type=MESH)

    scale_load = pltpu.make_async_copy(scale_in, r.scale.at[0], r.scale_sem.at[0])
    scale_load.start()
    owner_load = pltpu.make_async_copy(owner_in, r.owner, r.scale_sem.at[1])
    owner_load.start()

    def part(g, k, core):
        a = (centre[g][0] + OFFSETS[k]) % SIDE
        lines = pl.ds(HALF * g, HALF)
        return pay_in.at[a, :, core, lines] if g == 0 else pay_in.at[:, a, core, lines]

    loads = {
        (g, k): pltpu.make_async_copy(part(g, k, c), r.mine[g].at[k], r.load_sem.at[g, k])
        for k in range(4)
        for g in GROUPS
    }
    state_loads = [
        pltpu.make_async_copy(ref, r.state.at[i], r.state_sem.at[i])
        for i, ref in enumerate((master_in, one_in, two_in))
    ]
    for copy in list(loads.values()) + state_loads:
        copy.start()
    pl.semaphore_wait(barrier, len(greeted))

    scale_pair = pltpu.make_async_remote_copy(
        scale_in,
        r.scale.at[1],
        r.scale_sem.at[2],
        r.scale_sem.at[3],
        device_id=sibling,
        device_id_type=MESH,
    )
    scale_pair.start()
    pair = {}
    for k in range(4):
        for g in GROUPS:
            pair[g, k] = remote(
                part(g, k, 1 - c), r.take[g].at[k], r.pair_sem[g], k, k, sibling
            )
    for g in GROUPS:
        pair[g, 0].start()

    def tell(step):
        for way, device in ((0, above), (1, below)):
            if (way, step) != (0, 2):
                pl.semaphore_signal(
                    r.known.at[way, step], inc=1, device_id=device, device_id_type=MESH
                )

    def learn(step):
        for way in range(2):
            if (way, step) != (0, 2):
                pl.semaphore_wait(r.known.at[way, step], 1)

    tell(0)

    scale_load.wait()
    scale_pair.wait_recv()
    for k in range(1, 4):
        for g in GROUPS:
            pair[g, k].start()
    eye = (iota((128, 128), 0) == iota((128, 128), 1)).astype(BF16)
    for k in range(4):
        parts = []
        for core in range(2):
            whole = [r.scale[core, :, i, 128 * k : 128 * k + 128] for i in range(2)]
            for _ in range(3):
                near_by = [value.astype(BF16).astype(F32) for value in whole]
                whole = [value - close for value, close in zip(whole, near_by)]
                parts += near_by
            parts.append(jnp.zeros((KEYS - 60, 128), F32))
        turned = lax.dot_general(
            eye,
            jnp.concatenate(parts, axis=0).astype(BF16),
            (((1,), (1,)), ((), ())),
            preferred_element_type=F32,
        )
        r.keys[k] = turned.reshape(4, 2, ROWS, 2 * KEYS)

    unit = SIDE * HALF
    repeat = (iota((unit, 32), 0) // (2 * TILES) == iota((unit, 32), 1)).astype(BF16)
    line = iota((unit, 2 * KEYS), 0) % (2 * TILES)
    match = iota((unit, 2 * KEYS), 1) % KEYS % (2 * TILES) == line % 2 * TILES + line // 2
    ones = (iota((2 * KEYS, 256), 0) // KEYS == iota((2 * KEYS, 256), 1) // 128).astype(BF16)

    def terms(g, k):
        a = (centre[g][0] + OFFSETS[k]) % SIDE
        rows = slice(8 * g, 8 * g + 8)
        keys = r.keys[a, :, c, rows] if g == 0 else r.keys[:, a, c, rows]
        many = jnp.dot(repeat, keys.reshape(32, 2 * KEYS).astype(BF16), preferred_element_type=F32)
        many = jnp.where(match, many, 0.0).astype(BF16)
        scales = jnp.dot(many, ones, preferred_element_type=F32)
        loads[g, k].wait()
        pair[g, k].wait_recv()
        total = r.mine[g][k].astype(F32).reshape(unit, 128) * scales[:, :128]
        total += r.take[g][k].astype(F32).reshape(unit, 128) * scales[:, 128:]
        return total.reshape(SIDE, HALF, 128)

    first = {}
    lower, upper = slice(0, 2), slice(2, 4)

    def pass_on(g, number, source, target, step):
        first[g, number] = remote(
            source,
            target,
            r.first_sem[g],
            number,
            number,
            near(g, (centre[g][0] + step) % SIDE),
        )
        first[g, number].start()

    for g in GROUPS:
        r.first[g][0] = terms(g, 0).astype(BF16)
        sent_ref, relay = r.first[g].at[0], r.relay_in[g]
        pass_on(g, 0, sent_ref.at[pl.ds(0, 2)], relay.at[0], 1)
        pass_on(g, 1, sent_ref.at[pl.ds(2, 2)], relay.at[1], 3)
    for side, (k, step, now, later, start) in enumerate(
        ((1, 1, upper, lower, 2), (2, 3, lower, upper, 0))
    ):
        for g in GROUPS:
            total = terms(g, k)
            r.first[g][k, now] = total[now].astype(BF16)
            pass_on(
                g,
                2 + 2 * side,
                r.first[g].at[k, pl.ds(start, 2)],
                r.first_in[g].at[side, pl.ds(start, 2)],
                step,
            )
            r.hold[g][side] = total[later]
    for side, (k, step, later, start) in enumerate(((1, 1, lower, 0), (2, 3, upper, 2))):
        for g in GROUPS:
            first[g, side].wait_recv()
            r.first[g][k, later] = (
                r.hold[g][side] + r.relay_in[g][side].astype(F32)
            ).astype(BF16)
            pass_on(
                g,
                3 + 2 * side,
                r.first[g].at[k, pl.ds(start, 2)],
                r.first_in[g].at[side, pl.ds(start, 2)],
                step,
            )
    for g in GROUPS:
        r.own[g][...] = terms(g, 3)
    learn(0)
    tell(1)

    owner_load.wait()
    targets = r.owner[...].astype(F32)
    square = (ROWS, ROWS)
    diagonal = jnp.where(iota(square, 0) == iota(square, 1), jnp.broadcast_to(targets, square), 0.0)
    columns = jnp.dot(diagonal.astype(BF16), jnp.ones(square, BF16), preferred_element_type=F32)
    earlier = (columns == targets) & (iota(square, 0) < iota(square, 1))
    rank = jnp.sum(jnp.where(earlier, 1.0, 0.0), axis=0, keepdims=True)
    slot = jnp.broadcast_to(targets * 2.0 + rank, (8, ROWS)).astype(BF16)
    wide = (ROWS, LINES)
    stretch = (iota(wide, 1) // (2 * TILES) == iota(wide, 0)).astype(BF16)
    slot = jnp.dot(slot, stretch, preferred_element_type=F32)[0:1].astype(jnp.int32)
    line = iota((1, LINES), 1) % (2 * TILES)
    for h, (h0, n) in enumerate(CHUNKS):
        inside = (line >= 2 * h0) & (line < 2 * h0 + 2 * n)
        goal = jnp.where(inside, slot * (2 * n) + line - 2 * h0, -1)
        r.select[h][...] = (iota((128 * n, LINES), 0) == goal).astype(BF16)
    for copy in state_loads:
        copy.wait()

    learn(1)
    tell(2)

    second = {}
    for g in GROUPS:
        b0 = centre[g][1]
        for number in range(2, 6):
            first[g, number].wait_recv()
        for k in range(4):
            b = (b0 + OFFSETS[k]) % SIDE
            total = r.own[g][b]
            for j in range(2):
                total += r.first_in[g][j, b].astype(F32)
            if k == 3:
                r.total[g][...] = total
                continue
            r.second[g][k] = total.astype(BF16)
            second[g, k] = remote(
                r.second[g].at[k],
                r.second_in[g].at[k],
                r.second_sem[g],
                k,
                k,
                near(1 - g, b),
            )
            second[g, k].start()

    fix_one = 1.0 - 0.9 ** (STEP + 1)
    fix_two = 1.0 - 0.95 ** (STEP + 1)
    for g in GROUPS:
        for k in range(3):
            second[g, k].wait_recv()
        lines = slice(HALF * g, HALF * g + HALF)
        grad = r.total[g][...]
        for j in range(3):
            grad += r.second_in[g][j].astype(F32)
        master, one, two = (r.state[i, lines] for i in range(3))
        one = 0.9 * one + 0.1 * grad
        two = 0.95 * two + 0.05 * grad * grad
        direction = one * (1.0 / fix_one) / (jnp.sqrt(two * (1.0 / fix_two)) + 1e-08)
        master = master - 0.00015 * (direction + 0.1 * master)
        for i, value in enumerate((master, one, two)):
            r.fresh[i, lines] = value
        r.rounded[lines] = master.astype(BF16)
    spread = []
    for h, (_, n) in enumerate(CHUNKS):
        moved = jnp.dot(r.select[h][...], r.rounded[...], preferred_element_type=F32)
        r.slots[h][...] = moved.reshape(NDP, 4 * n, 128).astype(BF16)

        for i, j, core in AWAY:
            d = place((x + i) % SIDE, (y + j) % SIDE, (c + core) % 2)
            copy = remote(
                r.slots[h].at[d],
                r.plane[h].at[dp // 4, dp % 4],
                r.plane_sem[h],
                place(i, j, core),
                place(i, j, core),
                (d, z),
            )
            copy.start()
            spread.append(copy)
        pltpu.make_async_copy(
            r.slots[h].at[dp], r.plane[h].at[dp // 4, dp % 4], r.plane_sem[h].at[1, 0]
        ).start()
    fresh_store = pltpu.make_async_copy(r.fresh, fresh_out, r.fresh_sem)
    fresh_store.start()

    learn(2)
    deep = []

    def arrive(h, to):
        for i in range(4):
            source = 4 * to + i
            away = place(
                (x + SIDE - source // 8) % SIDE, (y + SIDE - source // 2 % SIDE) % SIDE, (c + source) % 2
            )
            slots = r.plane[h].at[to, i]
            pltpu.make_async_copy(slots, slots, r.plane_sem[h].at[1, away]).wait()

    for h, (_, n) in enumerate(CHUNKS):

        there = next_out[h].at[z]
        for i in (4, 3, 5, 2, 6, 1, 7):
            to = (z + i) % DEPTH
            arrive(h, to)
            copy = remote(r.plane[h].at[to], there, r.deep_sem[h], i, i, (dp, to))
            copy.start()
            deep.append(copy)
        arrive(h, z)
        copy = pltpu.make_async_copy(r.plane[h].at[z], there, r.deep_sem[h].at[0, 0])
        copy.start()
        deep.append(copy)
    for copy in [scale_pair] + list(pair.values()) + list(first.values()) + list(second.values()):
        copy.wait_send()
    for copy in spread:
        copy.wait_send()
    for copy in [fresh_store] + deep:
        copy.wait()


def finish(fresh, *rest):
    parts = len(CHUNKS)
    arrived, outs, rows_out = rest[:parts], rest[parts : parts + 3], rest[parts + 3]
    state_sem, rows_sem = rest[parts + 4 :]
    copies = [
        pltpu.make_async_copy(
            arrived[h].at[m], rows_out.at[:, pl.ds(m * TILES + h0, n)], rows_sem.at[h, m]
        )
        for h, (h0, n) in enumerate(CHUNKS)
        for m in range(DEPTH)
    ]
    copies += [pltpu.make_async_copy(fresh.at[i], outs[i], state_sem.at[i]) for i in range(3)]
    for copy in copies:
        copy.start()
    for copy in copies:
        copy.wait()


def body(payload, block_scale, master, moment_one, moment_two, owner):
    def plain(array):
        return with_layout_constraint(array, Layout(tuple(range(array.ndim))))

    def fold(array, shape):
        split = array.shape[:-1] + (array.shape[-1] // 128, 128)
        return plain(jnp.swapaxes(array.reshape(split), -3, -2)).reshape(shape)

    def unfold(array):
        array = jnp.swapaxes(array, -3, -2)
        return array.reshape(array.shape[:-2] + (-1,))

    anywhere = pl.BlockSpec(memory_space=pl.ANY)
    fresh, *arrived = pl.pallas_call(
        kernel,
        out_shape=(
            jax.ShapeDtypeStruct((3, LINES, 128), F32),
            *(jax.ShapeDtypeStruct((DEPTH, 4, 4 * n, 128), BF16) for _, n in CHUNKS),
        ),
        in_specs=[anywhere] * 6,
        out_specs=(anywhere,) * (1 + len(CHUNKS)),
        scratch_shapes=SCRATCH,
        compiler_params=pltpu.CompilerParams(
            collective_id=0, has_side_effects=True, vmem_limit_bytes=52 * 2**20
        ),
    )(
        *(pltpu.with_memory_space_constraint(array, pltpu.HBM) for array in (
        fold(payload[0], (SIDE, SIDE, 2, LINES, 128)),
        jnp.transpose(block_scale[0], (2, 1, 0)),
        fold(master, (LINES, 128)),
        fold(moment_one, (LINES, 128)),
        fold(moment_two, (LINES, 128)),
        owner.T,
        ))
    )
    state = jax.ShapeDtypeStruct((ROWS, TILES, 2, 128), F32)
    results = pl.pallas_call(
        finish,
        out_shape=(state, state, state, jax.ShapeDtypeStruct((8, DEPTH * TILES, 2, 128), BF16)),
        in_specs=[anywhere] * (1 + len(CHUNKS)),
        out_specs=(anywhere,) * 4,
        scratch_shapes=[
            pltpu.SemaphoreType.DMA((3,)),
            pltpu.SemaphoreType.DMA((len(CHUNKS), DEPTH)),
        ],
        compiler_params=pltpu.CompilerParams(vmem_limit_bytes=8 * 2**20),
    )(
        fresh.reshape(3, ROWS, TILES, 2, 128),
        *(part.reshape(DEPTH, 8, n, 2, 128) for part, (_, n) in zip(arrived, CHUNKS)),
    )
    return tuple(unfold(result) for result in results)


def solution(mesh):
    return jax.shard_map(
        body,
        mesh=mesh,
        in_specs=(
            P("dp", None, None, "mp"),
            P("dp", None, None, "mp"),
            P("dp", None, "mp"),
            P("dp", None, "mp"),
            P("dp", None, "mp"),
            P("dp", None),
        ),
        out_specs=(
            P("dp", None, "mp"),
            P("dp", None, "mp"),
            P("dp", None, "mp"),
            P(("dp", "mp"), None, None),
        ),
        check_vma=False,
    )
```
